256 devices in a mesh: row: 32 (over z, y_lo, core), col: 8 (over y_hi, x).
Axes of the slice: x: 4, y: 4 (y_hi: 2, y_lo: 2; y = y_hi * 2 + y_lo), z: 8, core: 2. Of those that a mesh axis runs over, the one named last changes fastest.
Arguments:
- sketches: float32 [10240, 4096], P(('row', 'col')), may hold values from -30 to 30
- targets: float32 [10240, 32], P(('row', 'col')), may hold values from -6 to 6
Outputs:
- weights: float32 [10240, 32], P(('row', 'col'))
- residual: float32 [10240, 32], P(('row', 'col'))
The draws below stay inside these ranges and needn't reach their ends.
All inputs are finite; a program needn't handle non-finite values.
Results may differ from the reference program's by a relative error of at most 0.0021.
The reference program's roundings to bfloat16 on the way (of `units`) count: a program that leaves them out, or rounds other values in their place, can miss the bound.
Values may be sent and summed in bfloat16 or wider, within the bound.
No kernel may reach another device: no remote copies, remote signals or barrier semaphores. Data moves between devices by JAX's collectives and lax.ppermute only.
A program may use at most 64 MiB of HBM per device.

```python
import math
import jax
import jax.numpy as jnp
from jax import lax

ROWS_DEV = 40
SKETCH = 4096
RHS = 32
ITERS = 2
CANDS = 10240
N_ROW = 32
N_COL = 8


def draw_sketches(key, part):
    key = jax.random.fold_in(key, 11)
    key_rows, key_noise = jax.random.split(key, 2)
    column_rank = jnp.arange(1, SKETCH + 1).astype(jnp.float32)
    spread = 1.5 * column_rank ** (-0.5)
    row_scale = jnp.exp(jax.random.uniform(key_rows, (CANDS, 1), jnp.float32, math.log(0.3), math.log(3.2)))
    entries = jnp.clip(jax.random.normal(key_noise, (CANDS, SKETCH), jnp.float32), -6.0, 6.0)
    return row_scale * spread[None, :] * entries


def levels(key, extent, cuts, low, high):
    def one(dim, blocks):
        draws = jax.random.uniform(jax.random.fold_in(jax.random.fold_in(key, 6), dim), (blocks,), jnp.float32, low / len(cuts), high / len(cuts))
        return jnp.repeat(jnp.exp(draws), extent[dim] // blocks).reshape((-1,) + (1,) * (len(extent) - dim - 1))

    gain = one(*cuts[0])
    for cut in cuts[1:]:
        gain = gain * one(*cut)
    return gain


def gaussian(stream_key, extent, deviation, bound, shards=(), dtype=jnp.bfloat16):
    loudness = levels(stream_key, extent, shards, -0.22, 0.18) if shards else 1.0
    drawn = jax.random.normal(stream_key, extent, jnp.float32) * deviation * loudness
    return jnp.minimum(jnp.maximum(drawn, -bound), bound).astype(dtype)


def setup_inputs(seed: int = 0) -> dict:
    arg_keys = jax.random.split(jax.random.key(seed), 3)
    sketches = draw_sketches(jax.random.fold_in(arg_keys[2], 71), 0)
    targets = gaussian(arg_keys[1], (CANDS, RHS), 1.0, 6.0, ((0, 256),), jnp.float32)
    return {"sketches": sketches, "targets": targets}


sharpness = 4.0
ridge = 1.0

def unit_rows(sketches):
    scale = jnp.sqrt(lax.optimization_barrier(jnp.sum(sketches * sketches, axis=1, keepdims=True)) + 1e-06)
    return (sketches / scale).astype(jnp.bfloat16)

def kernel_block(left, right):
    cosines = jnp.dot(left.astype(jnp.float32), right.T.astype(jnp.float32), preferred_element_type=jnp.float32)
    return jnp.exp(sharpness * (cosines - 1.0))

def gram(first, second):
    return jnp.dot(first.T, second, precision=lax.Precision.HIGHEST)

def solve_small(matrix, rhs_block):
    matrix = 0.5 * (matrix + matrix.T)
    factor = jnp.linalg.cholesky(matrix)
    return jax.scipy.linalg.cho_solve((factor, True), rhs_block)

def times_small(left, small):
    return jnp.dot(left, small, precision=lax.Precision.HIGHEST)

def reference(sketches, targets):
    units = unit_rows(sketches)
    blocks = units.reshape(N_ROW, ROWS_DEV * N_COL, SKETCH)
    kernel = lax.map(lambda block: kernel_block(block, units), blocks).reshape(CANDS, CANDS)

    def operate(vec):
        return jnp.dot(kernel, vec, precision=lax.Precision.HIGHEST) + ridge * vec
    weights = jnp.zeros_like(targets)
    residual = targets
    direction = targets
    norm_now = gram(residual, residual)
    for step in range(ITERS):
        image = operate(direction)
        alpha = solve_small(gram(direction, image), norm_now)
        weights = weights + times_small(direction, alpha)
        residual = residual - times_small(image, alpha)
        norm_next = gram(residual, residual)
        beta = solve_small(norm_now, norm_next)
        direction = residual + times_small(direction, beta)
        norm_now = norm_next
    return (weights, residual)
```

```python
import jax
import jax.numpy as jnp
from jax import lax
from jax.sharding import PartitionSpec as P

sharpness = 4.0
ridge = 1.0
AXES = ("row", "col")
NZ, NY, NX, NC = 8, 4, 4, 2
HIGH = lax.Precision.HIGHEST


def device(z, y, x, c):
    return ((z * 2 + y % 2) * 2 + c) * 8 + (y // 2) * 4 + x


LINES = [
    [device(z, y, x, c) for z in range(NZ)]
    for y in range(NY)
    for x in range(NX)
    for c in range(NC)
]
PLANES = [
    [device(z, y, x, c) for y in range(NY) for x in range(NX)]
    for z in range(NZ)
    for c in range(NC)
]
CORES = [
    (device(z, y, x, c), device(z, y, x, 1 - c))
    for z in range(NZ)
    for y in range(NY)
    for x in range(NX)
    for c in range(NC)
]


def unit_rows(sketches):
    scale = jnp.sqrt(jnp.sum(sketches * sketches, axis=1, keepdims=True) + 1e-06)
    return (sketches / scale).astype(jnp.bfloat16)


def mm(a, b):
    return jnp.dot(a, b, precision=HIGH)


def nt(a, b):
    return lax.dot_general(a, b, (((1,), (1,)), ((), ())), precision=HIGH)


def to_all(value, groups):
    size = len(groups[0])
    copies = jnp.broadcast_to(value[None], (size,) + value.shape)
    return lax.all_to_all(copies, AXES, 0, 0, axis_index_groups=groups, tiled=True)


def other_core(value):
    return lax.ppermute(value, AXES, CORES)


def solve_small(matrix, rhs_block):
    matrix = 0.5 * (matrix + matrix.T)
    factor = jnp.linalg.cholesky(matrix)
    return jax.scipy.linalg.cho_solve((factor, True), rhs_block)


def local(sketches, targets):
    units = unit_rows(sketches)
    rows, rhs = targets.shape
    line = NZ * rows
    z = lax.axis_index("row") // 4
    mine = lax.all_gather(units, AXES, axis=0, tiled=True, axis_index_groups=LINES)
    t_own = targets.T
    t_plane = to_all(t_own, PLANES)
    t_line = to_all(t_own, LINES)
    plane = to_all(units, PLANES).reshape(NY * NX * rows, -1)
    theirs = other_core(mine)

    def tile(left):
        cosines = lax.dot_general(
            plane, left, (((1,), (1,)), ((), ())), preferred_element_type=jnp.float32
        )
        return jnp.exp(sharpness * (cosines - 1.0))

    k_mine, k_theirs = tile(mine), tile(theirs)

    t_plane = t_plane.transpose(1, 0, 2).reshape(rhs, -1)
    t_line = t_line.transpose(1, 0, 2).reshape(rhs, -1)
    m0 = nt(t_plane, t_plane)

    part = jnp.concatenate([mm(t_plane, k_mine), m0], axis=1)
    away = jnp.concatenate([mm(t_plane, k_theirs), m0], axis=1)
    part = part + other_core(away)
    part = jnp.sum(to_all(part, LINES), axis=0)
    v1_line = part[:, :line] + ridge * t_line
    m0 = part[:, line:]

    m12 = jnp.concatenate([nt(t_line, v1_line), nt(v1_line, v1_line)], axis=1)
    far = other_core(jnp.concatenate([v1_line, m12], axis=1))
    v1_far = far[:, :line]
    m12 = m12 + far[:, line:]
    v1_own = lax.dynamic_slice(v1_line, (0, z * rows), (rhs, rows))
    got = to_all(jnp.concatenate([v1_own, m12], axis=1), PLANES)
    v1_plane = got[:, :, :rows].transpose(1, 0, 2).reshape(rhs, -1)
    m12 = jnp.sum(got[:, :, rows:], axis=0)
    m1, m2 = m12[:, :rhs], m12[:, rhs:]

    near2 = mm(v1_plane, k_mine)
    far2 = mm(v1_plane, k_theirs)
    m3 = nt(v1_line, near2) + nt(v1_far, far2)
    sent = other_core(jnp.concatenate([far2, m3], axis=1))
    near2 = near2 + sent[:, :line]
    m3 = m3 + sent[:, line:]
    chunks = near2.reshape(rhs, NZ, rows).transpose(1, 0, 2)
    chunks = jnp.concatenate([chunks, jnp.broadcast_to(m3[None], (NZ, rhs, rhs))], axis=2)
    chunks = jnp.sum(
        lax.all_to_all(chunks, AXES, 0, 0, axis_index_groups=LINES, tiled=True), axis=0
    )
    v2_own = chunks[:, :rows] + ridge * v1_own
    m3 = jnp.sum(to_all(chunks[:, rows:], PLANES), axis=0)
    m3 = m3 + ridge * m2

    a1 = solve_small(m1, m0)
    m1a = mm(m1, a1)
    rr1 = m0 - m1a - m1a.T + mm(a1.T, mm(m2, a1))
    e = jnp.eye(rhs, dtype=jnp.float32) + solve_small(m0, rr1)
    em2a = mm(e.T, mm(m2, a1))
    curve = mm(e.T, mm(m1, e)) - em2a - em2a.T + mm(a1.T, mm(m3, a1))
    a2 = solve_small(curve, rr1)
    direction = mm(e.T, t_own) - mm(a1.T, v1_own)
    image = mm(e.T, v1_own) - mm(a1.T, v2_own)
    weights = mm(a1.T, t_own) + mm(a2.T, direction)
    residual = t_own - mm(a1.T, v1_own) - mm(a2.T, image)
    return weights.T, residual.T


def solution(mesh):
    in_specs = (P(AXES, None), P(AXES, None))
    out_specs = (P(AXES, None), P(AXES, None))
    return jax.shard_map(local, mesh=mesh, in_specs=in_specs, out_specs=out_specs, check_vma=False)
```

```python
import functools

import jax
import jax.numpy as jnp
from jax import lax
from jax.experimental import pallas as pl
from jax.experimental.pallas import tpu as pltpu
from jax.sharding import PartitionSpec as P

sharpness = 4.0
AXES = ("row", "col")
NZ, NY, NX, NC = 8, 4, 4, 2
HIGH = lax.Precision.HIGHEST
PAD = 128


def device(z, y, x, c):
    z, y, x = z % NZ, y % NY, x % NX
    return ((z * 2 + y % 2) * 2 + c) * 8 + (y // 2) * 4 + x


PLACES = [
    (z, y, x, c) for z in range(NZ) for y in range(NY) for x in range(NX) for c in range(NC)
]
LINES = [
    [device(z, y, x, c) for z in range(NZ)]
    for y in range(NY)
    for x in range(NX)
    for c in range(NC)
]
PLANES = [
    [device(z, y, x, c) for y in range(NY) for x in range(NX)]
    for z in range(NZ)
    for c in range(NC)
]


def from_x(value, k):
    return lax.ppermute(
        value, AXES, [(device(z, y, x + k, c), device(z, y, x, c)) for z, y, x, c in PLACES]
    )


def from_y(value, k):
    return lax.ppermute(
        value, AXES, [(device(z, y + k, x, c), device(z, y, x, c)) for z, y, x, c in PLACES]
    )


def other_core(value):
    return lax.ppermute(
        value, AXES, [(device(z, y, x, 1 - c), device(z, y, x, c)) for z, y, x, c in PLACES]
    )


def mm(a, b):
    return jnp.dot(a, b, precision=HIGH, preferred_element_type=jnp.float32)


def nt(a, b):
    return lax.dot_general(
        a, b, (((1,), (1,)), ((), ())), precision=HIGH, preferred_element_type=jnp.float32
    )


def to_all(value, groups):
    size = len(groups[0])
    copies = jnp.broadcast_to(value[None], (size,) + value.shape)
    return lax.all_to_all(copies, AXES, 0, 0, axis_index_groups=groups, tiled=True)


def tile_kernel(rows, rhs, half, *refs):
    x_hbm, a_hbm, b_hbm = refs[0], refs[1:5], refs[5:9]
    k_ref, p_ref, tx_ref, ty_ref = refs[9:13]
    x_ref, a_ref, b_ref, cos_ref, sems = refs[13:]
    side = 4 * rows
    copies = []
    for i in range(4):
        at = pl.ds(i * side, side)
        copies.append(pltpu.make_async_copy(a_hbm[i], a_ref.at[at], sems.at[i]))
    x_copy = pltpu.make_async_copy(x_hbm, x_ref, sems.at[8])
    for i in range(4):
        at = pl.ds(i * side, side)
        copies.append(pltpu.make_async_copy(b_hbm[i], b_ref.at[at], sems.at[4 + i]))
    x_copy.start()
    for copy in copies:
        copy.start()
    x_copy.wait()
    for copy in copies[:4]:
        copy.wait()
    dims = (((1,), (1,)), ((), ()))
    k_ref[...] = lax.dot_general(
        a_ref[:, :half], x_ref[:, :half], dims, preferred_element_type=jnp.float32
    )
    for copy in copies[4:]:
        copy.wait()
    cos_ref[...] = lax.dot_general(
        b_ref[...], x_ref[:, half : 2 * half], dims, preferred_element_type=jnp.float32
    )
    for y in range(4):
        for x in range(4):
            at, other = pl.ds((4 * y + x) * rows, rows), pl.ds((4 * x + y) * rows, rows)
            k_ref[at, :] = jnp.exp(sharpness * (k_ref[at, :] + cos_ref[other, :] - 1.0))

    def targets(terms):
        terms = terms.astype(jnp.float32).T
        return terms[:rhs] + terms[rhs : 2 * rhs] + terms[2 * rhs : 3 * rhs]

    tx_ref[...] = targets(x_ref[:, 2 * half :])
    ty = targets(a_ref[:, half:])
    ty_ref[...] = ty
    p_ref[...] = mm(ty, k_ref[...])


def tile(rows, rhs, half, x, a, b):
    f32 = jnp.float32
    line, plane = x.shape[0], 16 * rows
    any_spec = pl.BlockSpec(memory_space=pl.ANY)
    vmem = pl.BlockSpec(memory_space=pltpu.VMEM)
    return pl.pallas_call(
        functools.partial(tile_kernel, rows, rhs, half),
        out_shape=(
            jax.ShapeDtypeStruct((plane, line), f32),
            jax.ShapeDtypeStruct((rhs, line), f32),
            jax.ShapeDtypeStruct((rhs, line), f32),
            jax.ShapeDtypeStruct((rhs, plane), f32),
        ),
        in_specs=[any_spec] * 9,
        out_specs=[vmem] * 4,
        scratch_shapes=[
            pltpu.VMEM((line, 2 * half + PAD), jnp.bfloat16),
            pltpu.VMEM((plane, half + PAD), jnp.bfloat16),
            pltpu.VMEM((plane, half), jnp.bfloat16),
            pltpu.VMEM((plane, line), f32),
            pltpu.SemaphoreType.DMA((9,)),
        ],
        compiler_params=pltpu.CompilerParams(vmem_limit_bytes=32 * 1024 * 1024),
        cost_estimate=pl.CostEstimate(
            flops=2 * plane * line * 2 * half,
            bytes_accessed=2 * (plane + line) * 2 * half,
            transcendentals=plane * line,
        ),
        name="tile",
    )(x, *a, *b)


def solve_small(matrix, rhs_block):
    matrix = 0.5 * (matrix + matrix.T)
    factor = jnp.linalg.cholesky(matrix)
    return jax.scipy.linalg.cho_solve((factor, True), rhs_block)


def local(sketches, targets):
    rows, rhs = targets.shape
    depth = sketches.shape[1]
    half = depth // 2
    line = NZ * rows
    z = lax.axis_index("row") // 4
    y = lax.axis_index("row") // 2 % 2 + 2 * (lax.axis_index("col") // NX)
    x = lax.axis_index("col") % NX
    bf16 = jnp.bfloat16

    scale = jnp.sqrt(jnp.sum(sketches * sketches, axis=1, keepdims=True) + 1e-06)
    units = (sketches / scale).astype(bf16)
    hi = targets.astype(bf16)
    rest = targets - hi.astype(jnp.float32)
    mid = rest.astype(bf16)
    low = (rest - mid.astype(jnp.float32)).astype(bf16)
    zero = jnp.zeros((rows, PAD - 3 * rhs), bf16)
    terms = jnp.concatenate([hi, mid, low, zero], axis=1)
    first = jnp.concatenate([units[:, :half], terms], axis=1)
    second = units[:, half:]

    mine = lax.all_gather(
        jnp.concatenate([units, terms], axis=1),
        AXES,
        axis=0,
        tiled=True,
        axis_index_groups=LINES,
    )
    a = jnp.concatenate([first] + [from_x(first, k) for k in range(1, NX)], axis=0)
    b = jnp.concatenate([second] + [from_y(second, k) for k in range(1, NY)], axis=0)
    a = [a] + [from_y(a, k) for k in range(1, NY)]
    b = [b] + [from_x(b, k) for k in range(1, NX)]
    theirs = other_core(mine)
    k_mine, p_mine, t_line, t_plane = tile(rows, rhs, half, mine, a, b)
    k_theirs, p_theirs, t_far, _ = tile(rows, rhs, half, theirs, a, b)

    n0 = nt(t_plane, t_plane)
    part = jnp.concatenate([p_mine, n0], axis=1)
    part = part + other_core(jnp.concatenate([p_theirs, n0], axis=1))
    part = jnp.sum(to_all(part, LINES), axis=0)
    w_line = part[:, :line] - t_line
    n0 = part[:, line:]

    n12 = jnp.concatenate([nt(t_line, w_line), nt(w_line, w_line)], axis=1)
    far = other_core(jnp.concatenate([w_line, n12], axis=1))
    w_far = far[:, :line]
    n12 = n12 + far[:, line:]
    w_own = lax.dynamic_slice(w_line, (0, z * rows), (rhs, rows))
    t_own = targets.T
    got = to_all(jnp.concatenate([w_own, n12], axis=1), PLANES)
    w_plane = got[:, :, :rows].reshape(NY, NX, rhs, rows)
    w_plane = lax.dynamic_slice_in_dim(jnp.concatenate([w_plane] * 2, axis=0), y, NY, 0)
    w_plane = lax.dynamic_slice_in_dim(jnp.concatenate([w_plane] * 2, axis=1), x, NX, 1)
    w_plane = w_plane.transpose(2, 0, 1, 3).reshape(rhs, -1)
    n12 = jnp.sum(got[:, :, rows:], axis=0)
    n1, n2 = n12[:, :rhs], n12[:, rhs:]

    eye = jnp.eye(rhs, dtype=jnp.float32)
    a1 = solve_small(n1 + 2.0 * n0, n0)
    q = eye - 2.0 * a1
    cross = mm(q.T, mm(n1, a1))
    rr1 = mm(q.T, mm(n0, q)) - cross - cross.T + mm(a1.T, mm(n2, a1))
    mix = (q + solve_small(n0, rr1)).T

    def direction(t, w):
        return mm(mix, t) - mm(a1.T, w)

    d_plane = direction(t_plane, w_plane)
    d_own = direction(t_own, w_own)
    near2 = mm(d_plane, k_mine)
    far2 = mm(d_plane, k_theirs)
    curve = nt(direction(t_line, w_line), near2) + nt(direction(t_far, w_far), far2)
    curve = curve + nt(d_own, d_own)
    sent = other_core(jnp.concatenate([far2, curve], axis=1))
    near2 = near2 + sent[:, :line]
    curve = curve + sent[:, line:]
    chunks = near2.reshape(rhs, NZ, rows).transpose(1, 0, 2)
    chunks = jnp.concatenate(
        [chunks, jnp.broadcast_to(curve[None], (NZ, rhs, rhs))], axis=2
    )
    chunks = jnp.sum(
        lax.all_to_all(chunks, AXES, 0, 0, axis_index_groups=LINES, tiled=True), axis=0
    )
    image = chunks[:, :rows] + d_own
    curve = jnp.sum(to_all(chunks[:, rows:], PLANES), axis=0)
    a2 = solve_small(curve, rr1)
    weights = mm(a1.T, t_own) + mm(a2.T, d_own)
    residual = mm(q.T, t_own) - mm(a1.T, w_own) - mm(a2.T, image)
    return weights.T, residual.T


def solution(mesh):
    in_specs = (P(AXES, None), P(AXES, None))
    out_specs = (P(AXES, None), P(AXES, None))
    return jax.shard_map(local, mesh=mesh, in_specs=in_specs, out_specs=out_specs, check_vma=False)
```

```python
import functools

import jax
import jax.numpy as jnp
from jax import lax
from jax.experimental import pallas as pl
from jax.experimental.pallas import tpu as pltpu
from jax.sharding import PartitionSpec as P

sharpness = 4.0
AXES = ("row", "col")
NZ, NY, NX, NC = 8, 4, 4, 2
HIGH = lax.Precision.HIGHEST
PAD = 128
VMEM = 48 * 1024 * 1024


def device(z, y, x, c):
    z, y, x = z % NZ, y % NY, x % NX
    return ((z * 2 + y % 2) * 2 + c) * 8 + (y // 2) * 4 + x


PLACES = [
    (z, y, x, c) for z in range(NZ) for y in range(NY) for x in range(NX) for c in range(NC)
]
LINES = [
    [device(z, y, x, c) for z in range(NZ)]
    for y in range(NY)
    for x in range(NX)
    for c in range(NC)
]
PLANES = [
    [device(z, y, x, c) for y in range(NY) for x in range(NX)]
    for z in range(NZ)
    for c in range(NC)
]


def from_x(value, k):
    return lax.ppermute(
        value, AXES, [(device(z, y, x + k, c), device(z, y, x, c)) for z, y, x, c in PLACES]
    )


def from_y(value, k):
    return lax.ppermute(
        value, AXES, [(device(z, y + k, x, c), device(z, y, x, c)) for z, y, x, c in PLACES]
    )


def other_core(value):
    return lax.ppermute(
        value, AXES, [(device(z, y, x, 1 - c), device(z, y, x, c)) for z, y, x, c in PLACES]
    )


def mm(a, b):
    return jnp.dot(a, b, precision=HIGH, preferred_element_type=jnp.float32)


def nt(a, b):
    return lax.dot_general(
        a, b, (((1,), (1,)), ((), ())), precision=HIGH, preferred_element_type=jnp.float32
    )


def to_all(value, groups):
    size = len(groups[0])
    copies = jnp.broadcast_to(value[None], (size,) + value.shape)
    return lax.all_to_all(copies, AXES, 0, 0, axis_index_groups=groups, tiled=True)


def tile_kernel(rows, rhs, half, *refs):
    x_hbm, a_hbm, b_hbm = refs[0:2], refs[2:6], refs[6:10]
    k_refs, p_refs, t_refs, ty_ref = refs[10:12], refs[12:14], refs[14:16], refs[16]
    x_ref, a_ref, b_ref, cos_ref, sems = refs[17:]
    side, line = 4 * rows, 8 * rows
    x_copies = [
        pltpu.make_async_copy(x_hbm[i], x_ref.at[pl.ds(i * line, line)], sems.at[i])
        for i in range(2)
    ]
    a_copies = [
        pltpu.make_async_copy(a_hbm[i], a_ref.at[pl.ds(i * side, side)], sems.at[2 + i])
        for i in range(4)
    ]
    b_copies = [
        pltpu.make_async_copy(b_hbm[i], b_ref.at[pl.ds(i * side, side)], sems.at[6 + i])
        for i in range(4)
    ]
    for copy in [x_copies[0]] + a_copies + b_copies + [x_copies[1]]:
        copy.start()

    def targets(terms):
        terms = terms.astype(jnp.float32).T
        return terms[:rhs] + terms[rhs : 2 * rhs] + terms[2 * rhs : 3 * rhs]

    dims = (((1,), (1,)), ((), ()))
    for i in range(2):
        at = pl.ds(i * line, line)
        k_ref = k_refs[i]
        x_copies[i].wait()
        if i == 0:
            for copy in a_copies:
                copy.wait()
            ty_ref[...] = targets(a_ref[:, half:])
        k_ref[...] = lax.dot_general(
            a_ref[:, :half], x_ref[at, :half], dims, preferred_element_type=jnp.float32
        )
        if i == 0:
            for copy in b_copies:
                copy.wait()
        cos_ref[...] = lax.dot_general(
            b_ref[...], x_ref[at, half : 2 * half], dims, preferred_element_type=jnp.float32
        )
        for y in range(4):
            for x in range(4):
                to, of = pl.ds((4 * y + x) * rows, rows), pl.ds((4 * x + y) * rows, rows)
                k_ref[to, :] = jnp.exp(sharpness * (k_ref[to, :] + cos_ref[of, :] - 1.0))
        t_refs[i][...] = targets(x_ref[at, 2 * half :])
        p_refs[i][...] = mm(ty_ref[...], k_ref[...])


def tile(rows, rhs, half, xs, a, b):
    f32 = jnp.float32
    line, plane = xs[0].shape[0], 16 * rows
    hbm = pl.BlockSpec(memory_space=pltpu.HBM)
    vmem = pl.BlockSpec(memory_space=pltpu.VMEM)
    return pl.pallas_call(
        functools.partial(tile_kernel, rows, rhs, half),
        out_shape=(jax.ShapeDtypeStruct((plane, line), f32),) * 2
        + (jax.ShapeDtypeStruct((rhs, line), f32),) * 4
        + (jax.ShapeDtypeStruct((rhs, plane), f32),),
        in_specs=[hbm] * 10,
        out_specs=[vmem] * 7,
        scratch_shapes=[
            pltpu.VMEM((2 * line, 2 * half + PAD), jnp.bfloat16),
            pltpu.VMEM((plane, half + PAD), jnp.bfloat16),
            pltpu.VMEM((plane, half), jnp.bfloat16),
            pltpu.VMEM((plane, line), f32),
            pltpu.SemaphoreType.DMA((10,)),
        ],
        compiler_params=pltpu.CompilerParams(vmem_limit_bytes=VMEM),
        cost_estimate=pl.CostEstimate(
            flops=4 * plane * line * 2 * half,
            bytes_accessed=2 * (plane + 2 * line) * 2 * half,
            transcendentals=2 * plane * line,
        ),
        name="tile",
    )(*xs, *a, *b)


def eliminate(pairs):
    size = pairs[0][0].shape[0]
    row = lax.broadcasted_iota(jnp.int32, (size, 1), 0)
    col = lax.broadcasted_iota(jnp.int32, (size, size), 1)
    pairs = list(pairs)
    for k in range(size):
        for n, (m, c) in enumerate(pairs):
            column = m[:, k : k + 1]
            factor = jnp.where(row == k, 0.0, column / m[k : k + 1, k : k + 1])
            pairs[n] = m - factor * m[k : k + 1, :], c - factor * c[k : k + 1, :]
    diagonal = lax.broadcasted_iota(jnp.int32, (size, size), 0) == col
    return [
        c / jnp.sum(jnp.where(diagonal, m, 0.0), axis=1, keepdims=True) for m, c in pairs
    ]


def symmetric(matrix):
    return 0.5 * (matrix + matrix.T)


def step_kernel(rows, rhs, *refs):
    at_ref, got_ref, n0_ref = refs[0:3]
    (w_line, w_far, w_own, t_line, t_far, t_own, k_mine, k_far, p_near, p_far) = refs[3:13]
    near_ref, far_ref, d_ref, weights_ref, residual_ref, rr_ref, w_ref = refs[13:]
    got = jnp.sum(got_ref[...], axis=0)
    n0 = symmetric(n0_ref[...])
    n1, n2 = got[:, rows : rows + rhs], got[:, rows + rhs : rows + 2 * rhs]
    y, x = at_ref[0], at_ref[1]
    for dy in range(4):
        for dx in range(4):
            s = 4 * dy + dx
            of = lax.rem(y + dy, 4) * 4 + lax.rem(x + dx, 4)
            w_ref[:, s * rows : (s + 1) * rows] = got_ref[of][:, :rows]
    kw_near, kw_far = mm(w_ref[...], k_mine[...]), mm(w_ref[...], k_far[...])
    eye = (
        lax.broadcasted_iota(jnp.int32, (rhs, rhs), 0)
        == lax.broadcasted_iota(jnp.int32, (rhs, rhs), 1)
    ).astype(jnp.float32)
    a1, n0_inverse = eliminate([(symmetric(n1) + 2.0 * n0, n0), (n0, eye)])
    a1t = a1.T
    q = eye - 2.0 * a1
    qt = eye - 2.0 * a1t
    cross = mm(qt, mm(n1, a1))
    rr1 = mm(qt, mm(n0, q)) - cross - cross.T + mm(a1t, mm(n2, a1))
    mix = qt + mm(n0_inverse, rr1).T
    d_own = mm(mix, t_own[...]) - mm(a1t, w_own[...])
    near = mm(mix, p_near[...]) - mm(a1t, kw_near)
    far = mm(mix, p_far[...]) - mm(a1t, kw_far)
    d_line = mm(mix, t_line[...]) - mm(a1t, w_line[...])
    d_far = mm(mix, t_far[...]) - mm(a1t, w_far[...])
    curve = nt(d_line, near) + nt(d_far, far) + nt(d_own, d_own)
    near_ref[...] = near
    line = near.shape[1]
    far_ref[:, :line] = far
    far_ref[:, line : line + rhs] = curve
    d_ref[...] = d_own
    weights_ref[...] = mm(a1t, t_own[...])
    residual_ref[...] = mm(qt, t_own[...]) - mm(a1t, w_own[...])
    rr_ref[...] = rr1


def step(rows, rhs, at, *values):
    f32 = jnp.float32
    line = values[2].shape[1]
    vmem = pl.BlockSpec(memory_space=pltpu.VMEM)
    own = jax.ShapeDtypeStruct((rhs, rows), f32)
    return pl.pallas_call(
        functools.partial(step_kernel, rows, rhs),
        out_shape=(
            jax.ShapeDtypeStruct((rhs, line), f32),
            jax.ShapeDtypeStruct((rhs, line + rhs), f32),
            own,
            own,
            own,
            jax.ShapeDtypeStruct((rhs, rhs), f32),
        ),
        in_specs=[pl.BlockSpec(memory_space=pltpu.SMEM)] + [vmem] * len(values),
        out_specs=[vmem] * 6,
        scratch_shapes=[pltpu.VMEM((rhs, 16 * rows), f32)],
        compiler_params=pltpu.CompilerParams(vmem_limit_bytes=VMEM),
        name="step",
    )(at, *values)


def last_kernel(rhs, got, rr, d_own, image, weights, residual, out_weights, out_residual):
    (a2,) = eliminate([(symmetric(jnp.sum(got[...], axis=0)), rr[...])])
    a2t = a2.T
    out_weights[...] = (weights[...] + mm(a2t, d_own[...])).T
    out_residual[...] = (residual[...] - mm(a2t, image[...])).T


def last(rows, rhs, *values):
    vmem = pl.BlockSpec(memory_space=pltpu.VMEM)
    return pl.pallas_call(
        functools.partial(last_kernel, rhs),
        out_shape=(jax.ShapeDtypeStruct((rows, rhs), jnp.float32),) * 2,
        in_specs=[vmem] * len(values),
        out_specs=[vmem] * 2,
        name="last",
    )(*values)


def local(sketches, targets):
    rows, rhs = targets.shape
    depth = sketches.shape[1]
    half = depth // 2
    line = NZ * rows
    z = lax.axis_index("row") // 4
    y = lax.axis_index("row") // 2 % 2 + 2 * (lax.axis_index("col") // NX)
    x = lax.axis_index("col") % NX
    bf16 = jnp.bfloat16

    scale = jnp.sqrt(jnp.sum(sketches * sketches, axis=1, keepdims=True) + 1e-06)
    units = (sketches / scale).astype(bf16)
    hi = targets.astype(bf16)
    rest = targets - hi.astype(jnp.float32)
    mid = rest.astype(bf16)
    low = (rest - mid.astype(jnp.float32)).astype(bf16)
    zero = jnp.zeros((rows, PAD - 3 * rhs), bf16)
    terms = jnp.concatenate([hi, mid, low, zero], axis=1)
    first = jnp.concatenate([units[:, :half], terms], axis=1)
    second = units[:, half:]

    mine = lax.all_gather(
        jnp.concatenate([units, terms], axis=1),
        AXES,
        axis=0,
        tiled=True,
        axis_index_groups=LINES,
    )
    a = jnp.concatenate([first] + [from_x(first, k) for k in range(1, NX)], axis=0)
    b = jnp.concatenate([second] + [from_y(second, k) for k in range(1, NY)], axis=0)
    a, b = lax.optimization_barrier((a, b))
    a = [a] + [from_y(a, k) for k in range(1, NY)]
    b = [b] + [from_x(b, k) for k in range(1, NX)]
    mine, a, b = lax.optimization_barrier((mine, a, b))
    theirs = other_core(mine)
    k_mine, k_far, p_mine, p_far, t_line, t_far, t_plane = tile(
        rows, rhs, half, (mine, theirs), a, b
    )

    n0 = nt(t_plane, t_plane)
    part = jnp.concatenate([p_mine, n0], axis=1)
    part = part + other_core(jnp.concatenate([p_far, n0], axis=1))
    part = jnp.sum(to_all(part, LINES), axis=0)
    w_line = part[:, :line] - t_line
    n0 = part[:, line:]

    n12 = jnp.concatenate([nt(t_line, w_line), nt(w_line, w_line)], axis=1)
    far = other_core(jnp.concatenate([w_line, n12], axis=1))
    w_far = far[:, :line]
    n12 = n12 + far[:, line:]
    w_own = lax.dynamic_slice(w_line, (0, z * rows), (rhs, rows))
    t_own = targets.T
    got = to_all(jnp.concatenate([w_own, n12], axis=1), PLANES)
    at = jnp.stack([y, x]).astype(jnp.int32)
    near2, away, d_own, weights, residual, rr1 = step(
        rows, rhs, at, got, n0, w_line, w_far, w_own, t_line, t_far, t_own, k_mine, k_far, p_mine, p_far
    )

    sent = other_core(away)
    near2 = near2 + sent[:, :line]
    chunks = near2.reshape(rhs, NZ, rows).transpose(1, 0, 2)
    curve = jnp.broadcast_to((away[:, line:] + sent[:, line:])[None], (NZ, rhs, rhs))
    chunks = jnp.concatenate([chunks, curve], axis=2)
    chunks = jnp.sum(
        lax.all_to_all(chunks, AXES, 0, 0, axis_index_groups=LINES, tiled=True), axis=0
    )
    image = chunks[:, :rows] + d_own
    got = to_all(chunks[:, rows:], PLANES)
    return last(rows, rhs, got, rr1, d_own, image, weights, residual)


def solution(mesh):
    in_specs = (P(AXES, None), P(AXES, None))
    out_specs = (P(AXES, None), P(AXES, None))
    return jax.shard_map(local, mesh=mesh, in_specs=in_specs, out_specs=out_specs, check_vma=False)
```

```python
import functools

import jax
import jax.numpy as jnp
from jax import lax
from jax.experimental import pallas as pl
from jax.experimental.pallas import tpu as pltpu
from jax.sharding import PartitionSpec as P

sharpness = 4.0
AXES = ("row", "col")
NZ, NY, NX, NC = 8, 4, 4, 2
HIGH = lax.Precision.HIGHEST
PAD = 128
MIB = 1024 * 1024
F32 = jnp.float32
BF16 = jnp.bfloat16
VM = pl.BlockSpec(memory_space=pltpu.VMEM)
SM = pl.BlockSpec(memory_space=pltpu.SMEM)
ANY = pl.BlockSpec(memory_space=pl.ANY)


def device(z, y, x, c):
    z, y, x = z % NZ, y % NY, x % NX
    return ((z * 2 + y % 2) * 2 + c) * 8 + (y // 2) * 4 + x


PLACES = [
    (z, y, x, c) for z in range(NZ) for y in range(NY) for x in range(NX) for c in range(NC)
]
LINES = [
    [device(z, y, x, c) for z in range(NZ)]
    for y in range(NY)
    for x in range(NX)
    for c in range(NC)
]
PLANES = [
    [device(z, y, x, c) for y in range(NY) for x in range(NX)]
    for z in range(NZ)
    for c in range(NC)
]


def from_x(value, k):
    return lax.ppermute(
        value, AXES, [(device(z, y, x + k, c), device(z, y, x, c)) for z, y, x, c in PLACES]
    )


def from_y(value, k):
    return lax.ppermute(
        value, AXES, [(device(z, y + k, x, c), device(z, y, x, c)) for z, y, x, c in PLACES]
    )


def other_core(value):
    return lax.ppermute(
        value, AXES, [(device(z, y, x, 1 - c), device(z, y, x, c)) for z, y, x, c in PLACES]
    )


def exchange(chunks, groups):
    return lax.all_to_all(chunks, AXES, 0, 0, axis_index_groups=groups, tiled=True)


def shape(*dims, dtype=F32):
    return jax.ShapeDtypeStruct(dims, dtype)


def mm(a, b):
    return jnp.dot(a, b, precision=HIGH, preferred_element_type=F32)


def nt(a, b):
    return lax.dot_general(
        a, b, (((1,), (1,)), ((), ())), precision=HIGH, preferred_element_type=F32
    )


def small_kernel(body, out, args, specs=None, limit=8, scratch=(), name=None):
    return pl.pallas_call(
        body,
        out_shape=out,
        in_specs=specs or [VM] * len(args),
        out_specs=jax.tree.map(lambda _: VM, out),
        scratch_shapes=list(scratch),
        compiler_params=pltpu.CompilerParams(vmem_limit_bytes=limit * MIB),
        name=name,
    )(*args)


def prepare_kernel(half, s_ref, t_ref, all_ref, first_ref, second_ref):
    sketches = s_ref[...]
    scale = jnp.sqrt(jnp.sum(sketches * sketches, axis=1, keepdims=True) + 1e-06)
    units = (sketches / scale).astype(BF16)
    targets = t_ref[...].T
    hi = targets.astype(BF16).astype(F32)
    mid = (targets - hi).astype(BF16).astype(F32)
    low = targets - hi - mid
    terms = jnp.concatenate([hi, mid, low, jnp.zeros_like(low)], axis=1).astype(BF16)
    all_ref[:, : 2 * half] = units
    all_ref[:, 2 * half :] = terms
    first_ref[:, :half] = units[:, :half]
    first_ref[:, half:] = terms
    second_ref[...] = units[:, half:]


def tile_body(rows, rhs, half, x_ref, a_ref, b_ref, cos_ref, k_ref):
    dims = (((1,), (1,)), ((), ()))
    k_ref[...] = lax.dot_general(
        a_ref[:, :half], x_ref[:, :half], dims, preferred_element_type=F32
    )
    cos_ref[...] = lax.dot_general(
        b_ref[...], x_ref[:, half : 2 * half], dims, preferred_element_type=F32
    )
    for y in range(4):
        for x in range(4):
            to, of = pl.ds((4 * y + x) * rows, rows), pl.ds((4 * x + y) * rows, rows)
            k_ref[to, :] = jnp.exp(sharpness * (k_ref[to, :] + cos_ref[of, :] - 1.0))


def targets_of(terms, rhs):
    terms = terms.astype(F32).T
    return terms[:rhs] + terms[rhs : 2 * rhs] + terms[2 * rhs : 3 * rhs]


def mine_kernel(rows, rhs, half, *refs):
    x_hbm, a_hbm, b_hbm = refs[0], refs[1:6], refs[6:11]
    k_ref, p_ref, tx_ref, ty_ref, n0_ref, a_ref, b_ref = refs[11:18]
    x_ref, cos_ref, sems = refs[18:]
    side, line = 4 * rows, 8 * rows
    places = [(0, side), (side, side), (2 * side, side // 2)]
    places += [(5 * side // 2, side // 2), (3 * side, side)]
    copies = [pltpu.make_async_copy(x_hbm, x_ref, sems.at[0])]
    for i, (at, size) in enumerate(places):
        to = pl.ds(at, size)
        copies.append(pltpu.make_async_copy(a_hbm[i], a_ref.at[to], sems.at[1 + 2 * i]))
        copies.append(pltpu.make_async_copy(b_hbm[i], b_ref.at[to], sems.at[2 + 2 * i]))
    for copy in copies:
        copy.start()
    for copy in copies:
        copy.wait()
    tile_body(rows, rhs, half, x_ref, a_ref, b_ref, cos_ref, k_ref)
    tx_ref[...] = targets_of(x_ref[:, 2 * half :], rhs)
    ty = targets_of(a_ref[:, half:], rhs)
    ty_ref[...] = ty
    n0 = nt(ty, ty)
    n0_ref[...] = n0
    p_ref[:, :line] = mm(ty, k_ref[...])
    p_ref[:, line:] = n0


def theirs_kernel(rows, rhs, half, *refs):
    x_hbm, a_ref, b_ref, ty_ref, n0_ref, k_ref, p_ref, tx_ref, x_ref, cos_ref, sem = refs
    line = 8 * rows
    copy = pltpu.make_async_copy(x_hbm, x_ref, sem)
    copy.start()
    copy.wait()
    tile_body(rows, rhs, half, x_ref, a_ref, b_ref, cos_ref, k_ref)
    tx_ref[...] = targets_of(x_ref[:, 2 * half :], rhs)
    p_ref[:, :line] = mm(ty_ref[...], k_ref[...])
    p_ref[:, line:] = n0_ref[...]


def share_kernel(count, a_ref, b_ref, out_ref):
    value = a_ref[...] + b_ref[...]
    for i in range(count):
        out_ref[i] = value


def line_kernel(line, part_ref, t_ref, send_ref, n0_ref):
    part = jnp.sum(part_ref[...], axis=0)
    rhs = part.shape[0]
    t = t_ref[...]
    w = part[:, :line] - t
    n0_ref[...] = part[:, line:]
    send_ref[:, :line] = w
    send_ref[:, line : line + rhs] = nt(t, w)
    send_ref[:, line + rhs :] = nt(w, w)


def spread_kernel(rows, line, at_ref, near_ref, far_ref, out_ref):
    grams = near_ref[:, line:] + far_ref[:, line:]
    own = jnp.zeros((near_ref.shape[0], rows), F32)
    for z in range(NZ):
        own = jnp.where(at_ref[0] == z, near_ref[:, z * rows : (z + 1) * rows], own)
    for i in range(NY * NX):
        out_ref[i, :, :rows] = own
        out_ref[i, :, rows:] = grams


def eliminate(pairs):
    size = pairs[0][0].shape[0]
    row = lax.broadcasted_iota(jnp.int32, (size, size), 0)
    col = lax.broadcasted_iota(jnp.int32, (size, size), 1)
    pairs = list(pairs)
    for k in range(size):
        for n, (m, c) in enumerate(pairs):
            column = jnp.broadcast_to(m[:, k : k + 1], (size, size))
            inverse = 1.0 / column[k : k + 1, :]
            column = jnp.where(row == k, 0.0, column)
            m_row, c_row = m[k : k + 1, :] * inverse, c[k : k + 1, :] * inverse
            pairs[n] = m - column * m_row, c - column * c_row
    return [
        c / jnp.sum(jnp.where(row == col, m, 0.0), axis=1, keepdims=True) for m, c in pairs
    ]


def symmetric(matrix):
    return 0.5 * (matrix + matrix.T)


def step_kernel(rows, rhs, line, at_ref, *refs):
    got_ref, n0_ref, w_line, w_far, t_line, t_far, t_plane, k_mine, k_far = refs[:9]
    near_ref, far_ref, d_ref, weights_ref, residual_ref, rr_ref, w_ref = refs[9:]
    got = jnp.sum(got_ref[...], axis=0)
    n0 = symmetric(n0_ref[...])
    n1, n2 = got[:, rows : rows + rhs], got[:, rows + rhs : rows + 2 * rhs]
    y, x = at_ref[1], at_ref[2]
    for dy in range(NY):
        for dx in range(NX):
            s = NX * dy + dx
            of = lax.rem(y + dy, NY) * NX + lax.rem(x + dx, NX)
            w_ref[:, s * rows : (s + 1) * rows] = got_ref[of][:, :rows]
    eye = (
        lax.broadcasted_iota(jnp.int32, (rhs, rhs), 0)
        == lax.broadcasted_iota(jnp.int32, (rhs, rhs), 1)
    ).astype(F32)
    a1, n0_inverse = eliminate([(symmetric(n1) + 2.0 * n0, n0), (n0, eye)])
    a1t = a1.T
    q = eye - 2.0 * a1
    qt = eye - 2.0 * a1t
    cross = mm(qt, mm(n1, a1))
    rr1 = mm(qt, mm(n0, q)) - cross - cross.T + mm(a1t, mm(n2, a1))
    mix = qt + mm(n0_inverse, rr1).T
    d_plane = mm(mix, t_plane[...]) - mm(a1t, w_ref[...])
    near = mm(d_plane, k_mine[...])
    far = mm(d_plane, k_far[...])
    d_line = mm(mix, t_line[...]) - mm(a1t, w_line[:, :line])
    d_far = mm(mix, t_far[...]) - mm(a1t, w_far[:, :line])
    d_own, t_own = d_plane[:, :rows], t_plane[:, :rows]
    near_ref[...] = near
    far_ref[:, :line] = far
    far_ref[:, line:] = nt(d_line, near) + nt(d_far, far) + nt(d_own, d_own)
    d_ref[...] = d_own
    weights_ref[...] = mm(a1t, t_own)
    residual_ref[...] = mm(qt, t_own) - mm(a1t, w_ref[:, :rows])
    rr_ref[...] = rr1


def chunk_kernel(rows, line, near_ref, far_ref, here_ref, out_ref):
    gram = far_ref[:, line:] + here_ref[:, line:]
    total = near_ref[...] + far_ref[:, :line]
    for z in range(NZ):
        out_ref[z, :, :rows] = total[:, z * rows : (z + 1) * rows]
        out_ref[z, :, rows:] = gram


def image_kernel(rows, got_ref, d_ref, image_ref, out_ref):
    got = jnp.sum(got_ref[...], axis=0)
    image_ref[...] = got[:, :rows] + d_ref[...]
    gram = got[:, rows:]
    dense = jnp.concatenate([gram[8 * i : 8 * i + 8] for i in range(4)], axis=1)
    for i in range(NY * NX):
        out_ref[i] = dense


def last_kernel(rhs, got_ref, rr, d_own, image, weights, residual, out_weights, out_residual):
    dense = jnp.sum(got_ref[...], axis=0)
    gram = jnp.concatenate([dense[:, rhs * i : rhs * (i + 1)] for i in range(4)], axis=0)
    (a2,) = eliminate([(symmetric(gram), rr[...])])
    a2t = a2.T
    out_weights[...] = weights[...] + mm(a2t, d_own[...])
    out_residual[...] = residual[...] - mm(a2t, image[...])


def local(sketches, targets):
    rows, rhs = targets.shape
    half = sketches.shape[1] // 2
    line, plane = NZ * rows, NY * NX * rows
    z = lax.axis_index("row") // 4
    y = lax.axis_index("row") // 2 % 2 + 2 * (lax.axis_index("col") // NX)
    x = lax.axis_index("col") % NX
    at = jnp.stack([z, y, x]).astype(jnp.int32)
    sizes = (rows, rhs, half)

    units, first, second = small_kernel(
        functools.partial(prepare_kernel, half),
        (
            shape(rows, 2 * half + PAD, dtype=BF16),
            shape(rows, half + PAD, dtype=BF16),
            shape(rows, half, dtype=BF16),
        ),
        (sketches, targets.T),
        name="prepare",
    )
    mine = lax.all_gather(units, AXES, axis=0, tiled=True, axis_index_groups=LINES)
    a = jnp.concatenate([first] + [from_x(first, k) for k in range(1, NX)], axis=0)
    b = jnp.concatenate([second] + [from_y(second, k) for k in range(1, NY)], axis=0)
    a, b = lax.optimization_barrier((a, b))
    a1, b1, a3, b3 = from_y(a, 1), from_x(b, 1), from_y(a, 3), from_x(b, 3)
    top = 2 * rows
    a2, b2 = from_y(a1[:top], 1), from_x(b1[:top], 1)
    a2_low, b2_low = from_y(a3[top:], 3), from_x(b3[top:], 3)
    mine, a, b = lax.optimization_barrier(
        (mine, (a, a1, a2, a2_low, a3), (b, b1, b2, b2_low, b3))
    )
    theirs = other_core(mine)
    cost = pl.CostEstimate(
        flops=4 * plane * line * half,
        bytes_accessed=2 * (plane + line) * 2 * half,
        transcendentals=plane * line,
    )
    k_mine, near, t_line, t_plane, n0, y_first, y_second = pl.pallas_call(
        functools.partial(mine_kernel, *sizes),
        out_shape=(
            shape(plane, line),
            shape(rhs, line + rhs),
            shape(rhs, line),
            shape(rhs, plane),
            shape(rhs, rhs),
            shape(plane, half + PAD, dtype=BF16),
            shape(plane, half, dtype=BF16),
        ),
        in_specs=[ANY] * 11,
        out_specs=[VM] * 7,
        scratch_shapes=[
            pltpu.VMEM((line, 2 * half + PAD), BF16),
            pltpu.VMEM((plane, line), F32),
            pltpu.SemaphoreType.DMA((11,)),
        ],
        compiler_params=pltpu.CompilerParams(vmem_limit_bytes=20 * MIB),
        cost_estimate=cost,
        name="tile_mine",
    )(mine, *a, *b)
    k_far, far, t_far = pl.pallas_call(
        functools.partial(theirs_kernel, *sizes),
        out_shape=(shape(plane, line), shape(rhs, line + rhs), shape(rhs, line)),
        in_specs=[ANY] + [VM] * 4,
        out_specs=[VM] * 3,
        scratch_shapes=[
            pltpu.VMEM((line, 2 * half + PAD), BF16),
            pltpu.VMEM((plane, line), F32),
            pltpu.SemaphoreType.DMA,
        ],
        compiler_params=pltpu.CompilerParams(vmem_limit_bytes=20 * MIB),
        cost_estimate=cost,
        name="tile_theirs",
    )(theirs, y_first, y_second, t_plane, n0)

    copies = small_kernel(
        functools.partial(share_kernel, NZ),
        shape(NZ, rhs, line + rhs),
        (near, other_core(far)),
        name="share",
    )
    sent, n0 = small_kernel(
        functools.partial(line_kernel, line),
        (shape(rhs, line + 2 * rhs), shape(rhs, rhs)),
        (exchange(copies, LINES), t_line),
        name="line",
    )
    received = other_core(sent)
    copies = small_kernel(
        functools.partial(spread_kernel, rows, line),
        shape(NY * NX, rhs, rows + 2 * rhs),
        (at, sent, received),
        [SM, VM, VM],
        name="spread",
    )
    got = exchange(copies, PLANES)
    own = shape(rhs, rows)
    values = (at, got, n0, sent, received, t_line, t_far, t_plane, k_mine, k_far)
    near, far, d_own, weights, residual, rr1 = small_kernel(
        functools.partial(step_kernel, rows, rhs, line),
        (shape(rhs, line), shape(rhs, line + rhs), own, own, own, shape(rhs, rhs)),
        values,
        [SM] + [VM] * 9,
        limit=16,
        scratch=[pltpu.VMEM((rhs, plane), F32)],
        name="step",
    )
    return finish(rows, rhs, line, near, far, d_own, weights, residual, rr1)


def finish(rows, rhs, line, near, far, d_own, weights, residual, rr1):
    away = other_core(far)
    chunks = small_kernel(
        functools.partial(chunk_kernel, rows, line),
        shape(NZ, rhs, rows + rhs),
        (near, away, far),
        name="chunk",
    )
    own = shape(rhs, rows)
    image, copies = small_kernel(
        functools.partial(image_kernel, rows),
        (own, shape(NY * NX, rhs // 4, 4 * rhs)),
        (exchange(chunks, LINES), d_own),
        name="image",
    )
    weights, residual = small_kernel(
        functools.partial(last_kernel, rhs),
        (own, own),
        (exchange(copies, PLANES), rr1, d_own, image, weights, residual),
        name="last",
    )
    return weights.T, residual.T


def solution(mesh):
    in_specs = (P(AXES, None), P(AXES, None))
    out_specs = (P(AXES, None), P(AXES, None))
    return jax.shard_map(local, mesh=mesh, in_specs=in_specs, out_specs=out_specs, check_vma=False)
```

```python
import functools

import jax
import jax.numpy as jnp
from jax import lax
from jax.experimental import pallas as pl
from jax.experimental.pallas import tpu as pltpu
from jax.sharding import PartitionSpec as P

sharpness = 4.0
AXES = ("row", "col")
NZ, NY, NX, NC = 8, 4, 4, 2
HIGH = lax.Precision.HIGHEST
PAD = 128
MIB = 1024 * 1024
F32 = jnp.float32
BF16 = jnp.bfloat16
VM = pl.BlockSpec(memory_space=pltpu.VMEM)
SM = pl.BlockSpec(memory_space=pltpu.SMEM)
HBM = pl.BlockSpec(memory_space=pltpu.HBM)


def device(z, y, x, c):
    z, y, x = z % NZ, y % NY, x % NX
    return ((z * 2 + y % 2) * 2 + c) * 8 + (y // 2) * 4 + x


PLACES = [
    (z, y, x, c) for z in range(NZ) for y in range(NY) for x in range(NX) for c in range(NC)
]
LINES = [
    [device(z, y, x, c) for z in range(NZ)]
    for y in range(NY)
    for x in range(NX)
    for c in range(NC)
]
TUBES = [
    [device(z, y, x, c) for c in range(NC) for z in range(NZ)]
    for y in range(NY)
    for x in range(NX)
]
PLANES = [
    [device(z, y, x, c) for y in range(NY) for x in range(NX)]
    for z in range(NZ)
    for c in range(NC)
]


def from_x(value, k):
    return lax.ppermute(
        value, AXES, [(device(z, y, x + k, c), device(z, y, x, c)) for z, y, x, c in PLACES]
    )


def from_y(value, k):
    return lax.ppermute(
        value, AXES, [(device(z, y + k, x, c), device(z, y, x, c)) for z, y, x, c in PLACES]
    )


def other_core(value):
    return lax.ppermute(
        value, AXES, [(device(z, y, x, 1 - c), device(z, y, x, c)) for z, y, x, c in PLACES]
    )


def exchange(chunks, groups):
    return lax.all_to_all(chunks, AXES, 0, 0, axis_index_groups=groups, tiled=True)


def shape(*dims, dtype=F32):
    return jax.ShapeDtypeStruct(dims, dtype)


def mm(a, b):
    return jnp.dot(a, b, precision=HIGH, preferred_element_type=F32)


def nt(a, b):
    return lax.dot_general(
        a, b, (((1,), (1,)), ((), ())), precision=HIGH, preferred_element_type=F32
    )


def small_kernel(body, out, args, specs=None, limit=8, scratch=(), name=None):
    return pl.pallas_call(
        body,
        out_shape=out,
        in_specs=specs or [VM] * len(args),
        out_specs=jax.tree.map(lambda _: VM, out),
        scratch_shapes=list(scratch),
        compiler_params=pltpu.CompilerParams(vmem_limit_bytes=limit * MIB),
        name=name,
    )(*args)


def prepare_kernel(half, s_hbm, t_hbm, all_ref, first_ref, second_ref, s_ref, t_ref, sems):
    copies = [
        pltpu.make_async_copy(t_hbm, t_ref, sems.at[1]),
        pltpu.make_async_copy(s_hbm, s_ref, sems.at[0]),
    ]
    for copy in copies:
        copy.start()
    for copy in copies:
        copy.wait()
    sketches = s_ref[...]
    scale = jnp.sqrt(jnp.sum(sketches * sketches, axis=1, keepdims=True) + 1e-06)
    units = (sketches / scale).astype(BF16)
    targets = t_ref[...].T
    hi = targets.astype(BF16).astype(F32)
    mid = (targets - hi).astype(BF16).astype(F32)
    low = targets - hi - mid
    terms = jnp.concatenate([hi, mid, low, jnp.zeros_like(low)], axis=1).astype(BF16)
    all_ref[:, : 2 * half] = units
    all_ref[:, 2 * half :] = terms
    first_ref[:, :half] = units[:, :half]
    first_ref[:, half:] = terms
    second_ref[...] = units[:, half:]


def spans(rows):
    side = 4 * rows
    return [
        pl.ds(at, size)
        for at, size in (
            (0, side),
            (side, side),
            (2 * side, side // 2),
            (5 * side // 2, side // 2),
            (3 * side, side),
        )
    ]


def targets_of(terms, rhs):
    terms = terms.astype(F32).T
    return terms[:rhs] + terms[rhs : 2 * rhs] + terms[2 * rhs : 3 * rhs]


def tile_kernel(rows, rhs, half, at_ref, *refs):
    x_hbm, a_hbm, b_hbm = refs[0], refs[1:6], refs[6:11]
    k_ref, near_ref, far_ref, tx_ref, ty_ref, n0_ref = refs[11:17]
    x_ref, a_ref, b_ref, cos_ref, sems = refs[17:]
    line, quarter = 8 * rows, half // 2
    dims = (((1,), (1,)), ((), ()))
    plans = (
        (0, quarter, a_hbm, a_ref, 0, quarter),
        (quarter, quarter, a_hbm, a_ref, quarter, quarter + PAD),
        (half, quarter, b_hbm, b_ref, 0, quarter),
        (half + quarter, quarter + PAD, b_hbm, b_ref, quarter, quarter),
    )
    groups = []
    for i, (at_x, wide_x, pieces, ref, at_y, wide_y) in enumerate(plans):
        group = []
        of_x, of_y = pl.ds(at_x, wide_x), pl.ds(at_y, wide_y)
        for core in range(NC):
            of = pl.multiple_of(lax.rem(at_ref[3] + core, NC) * line, line)
            copy = pltpu.make_async_copy(
                x_hbm.at[pl.ds(of, line), of_x],
                x_ref.at[pl.ds(core * line, line), of_x],
                sems.at[i, core],
            )
            group.append(copy)
        for n, (to, piece) in enumerate(zip(spans(rows), pieces)):
            group.append(
                pltpu.make_async_copy(piece.at[:, of_y], ref.at[to, of_y], sems.at[i, NC + n])
            )
        groups.append(group)
        for copy in group:
            copy.start()
    for i, (at_x, _, _, ref, at_y, _) in enumerate(plans):
        for copy in groups[i]:
            copy.wait()
        product = lax.dot_general(
            ref[:, at_y : at_y + quarter],
            x_ref[:, at_x : at_x + quarter],
            dims,
            preferred_element_type=F32,
        )
        to = k_ref if i < 2 else cos_ref
        if i % 2:
            to[...] += product
        else:
            to[...] = product
        if i == 1:
            ty = targets_of(a_ref[:, half:], rhs)
            ty_ref[...] = ty
            n0 = nt(ty, ty)
            n0_ref[...] = n0
            near_ref[:, line:] = n0
            far_ref[:, line:] = n0
    for y in range(4):
        for x in range(4):
            to, of = pl.ds((4 * y + x) * rows, rows), pl.ds((4 * x + y) * rows, rows)
            k_ref[to, :] = jnp.exp(sharpness * (k_ref[to, :] + cos_ref[of, :] - 1.0))
    tx_ref[...] = targets_of(x_ref[:, 2 * half :], rhs)
    product = mm(ty_ref[...], k_ref[...])
    near_ref[:, :line] = product[:, :line]
    far_ref[:, :line] = product[:, line:]


def share_kernel(count, a_ref, b_ref, out_ref):
    value = a_ref[...] + b_ref[...]
    for i in range(count):
        out_ref[i] = value


def line_kernel(line, part_ref, t_ref, send_ref, n0_ref):
    part = jnp.sum(part_ref[...], axis=0)
    rhs = part.shape[0]
    t = t_ref[:, :line]
    w = part[:, :line] - t
    n0_ref[...] = part[:, line:]
    send_ref[:, :line] = w
    send_ref[:, line : line + rhs] = nt(t, w)
    send_ref[:, line + rhs :] = nt(w, w)


def spread_kernel(rows, line, at_ref, near_ref, far_ref, out_ref):
    grams = near_ref[:, line:] + far_ref[:, line:]
    own = jnp.zeros((near_ref.shape[0], rows), F32)
    for z in range(NZ):
        own = jnp.where(at_ref[0] == z, near_ref[:, z * rows : (z + 1) * rows], own)
    for i in range(NY * NX):
        out_ref[i, :, :rows] = own
        out_ref[i, :, rows:] = grams


def eliminate(pairs):
    size = pairs[0][0].shape[0]
    row = lax.broadcasted_iota(jnp.int32, (size, size), 0)
    col = lax.broadcasted_iota(jnp.int32, (size, size), 1)
    pairs = list(pairs)
    block = 8
    for start in range(0, size, block):
        panels = [
            [
                jnp.broadcast_to(m[:, start + j : start + j + 1], (size, size))
                for j in range(block)
            ]
            for m, _ in pairs
        ]
        for j in range(block):
            k = start + j
            for n, (m, c) in enumerate(pairs):
                panel = panels[n]
                inverse = 1.0 / panel[j][k : k + 1, :]
                column = jnp.where(row == k, 0.0, panel[j])
                m_row, c_row = m[k : k + 1, :] * inverse, c[k : k + 1, :] * inverse
                pairs[n] = m - column * m_row, c - column * c_row
                for i in range(j + 1, block):
                    panel[i] = panel[i] - column * (panel[i][k : k + 1, :] * inverse)
    return [
        c / jnp.sum(jnp.where(row == col, m, 0.0), axis=1, keepdims=True) for m, c in pairs
    ]


def symmetric(matrix):
    return 0.5 * (matrix + matrix.T)


def step_kernel(rows, rhs, line, at_ref, *refs):
    got_ref, n0_ref, w_line, w_far, t_tube, t_plane, k_ref = refs[:7]
    near_ref, far_ref, d_ref, weights_ref, residual_ref, rr_ref, w_ref = refs[7:]
    got = jnp.sum(got_ref[...], axis=0)
    n0 = symmetric(n0_ref[...])
    n1, n2 = got[:, rows : rows + rhs], got[:, rows + rhs : rows + 2 * rhs]
    y, x = at_ref[1], at_ref[2]
    for dy in range(NY):
        for dx in range(NX):
            s = NX * dy + dx
            of = lax.rem(y + dy, NY) * NX + lax.rem(x + dx, NX)
            w_ref[:, s * rows : (s + 1) * rows] = got_ref[of][:, :rows]
    eye = (
        lax.broadcasted_iota(jnp.int32, (rhs, rhs), 0)
        == lax.broadcasted_iota(jnp.int32, (rhs, rhs), 1)
    ).astype(F32)
    a1, n0_inverse = eliminate([(symmetric(n1) + 2.0 * n0, n0), (n0, eye)])
    a1t = a1.T
    q = eye - 2.0 * a1
    qt = eye - 2.0 * a1t
    cross = mm(qt, mm(n1, a1))
    rr1 = mm(qt, mm(n0, q)) - cross - cross.T + mm(a1t, mm(n2, a1))
    mix = qt + mm(n0_inverse, rr1).T
    d_plane = mm(mix, t_plane[...]) - mm(a1t, w_ref[...])
    product = mm(d_plane, k_ref[...])
    near, far = product[:, :line], product[:, line:]
    d_line = mm(mix, t_tube[:, :line]) - mm(a1t, w_line[:, :line])
    d_far = mm(mix, t_tube[:, line:]) - mm(a1t, w_far[:, :line])
    d_own, t_own = d_plane[:, :rows], t_plane[:, :rows]
    near_ref[...] = near
    far_ref[:, :line] = far
    far_ref[:, line:] = nt(d_line, near) + nt(d_far, far) + nt(d_own, d_own)
    d_ref[...] = d_own
    weights_ref[...] = mm(a1t, t_own)
    residual_ref[...] = mm(qt, t_own) - mm(a1t, w_ref[:, :rows])
    rr_ref[...] = rr1


def chunk_kernel(rows, line, near_ref, far_ref, here_ref, out_ref):
    gram = far_ref[:, line:] + here_ref[:, line:]
    total = near_ref[...] + far_ref[:, :line]
    for z in range(NZ):
        out_ref[z, :, :rows] = total[:, z * rows : (z + 1) * rows]
        out_ref[z, :, rows:] = gram


def image_kernel(rows, got_ref, d_ref, image_ref, out_ref):
    got = jnp.sum(got_ref[...], axis=0)
    image_ref[...] = got[:, :rows] + d_ref[...]
    gram = got[:, rows:]
    dense = jnp.concatenate([gram[8 * i : 8 * i + 8] for i in range(4)], axis=1)
    for i in range(NY * NX):
        out_ref[i] = dense


def last_kernel(rhs, got_ref, rr, d_own, image, weights, residual, out_weights, out_residual):
    dense = jnp.sum(got_ref[...], axis=0)
    gram = jnp.concatenate([dense[:, rhs * i : rhs * (i + 1)] for i in range(4)], axis=0)
    (a2,) = eliminate([(symmetric(gram), rr[...])])
    a2t = a2.T
    out_weights[...] = weights[...] + mm(a2t, d_own[...])
    out_residual[...] = residual[...] - mm(a2t, image[...])


def local(sketches, targets):
    rows, rhs = targets.shape
    half = sketches.shape[1] // 2
    line, plane = NZ * rows, NY * NX * rows
    z = lax.axis_index("row") // 4
    y = lax.axis_index("row") // 2 % 2 + 2 * (lax.axis_index("col") // NX)
    x = lax.axis_index("col") % NX
    c = lax.axis_index("row") % NC
    at = jnp.stack([z, y, x, c]).astype(jnp.int32)
    sizes = (rows, rhs, half)

    units, first, second = small_kernel(
        functools.partial(prepare_kernel, half),
        (
            shape(rows, 2 * half + PAD, dtype=BF16),
            shape(rows, half + PAD, dtype=BF16),
            shape(rows, half, dtype=BF16),
        ),
        (sketches, targets.T),
        [HBM] * 2,
        scratch=[
            pltpu.VMEM((rows, 2 * half), F32),
            pltpu.VMEM((rhs, rows), F32),
            pltpu.SemaphoreType.DMA((2,)),
        ],
        name="prepare",
    )
    tube = lax.all_gather(units, AXES, axis=0, tiled=True, axis_index_groups=TUBES)
    a = jnp.concatenate([first] + [from_x(first, k) for k in range(1, NX)], axis=0)
    b = jnp.concatenate([second] + [from_y(second, k) for k in range(1, NY)], axis=0)
    a, b = lax.optimization_barrier((a, b))
    a1, b1, a3, b3 = from_y(a, 1), from_x(b, 1), from_y(a, 3), from_x(b, 3)
    top = 2 * rows
    a2, b2 = from_y(a1[:top], 1), from_x(b1[:top], 1)
    a2_low, b2_low = from_y(a3[top:], 3), from_x(b3[top:], 3)
    a, b = (a, a1, a2, a2_low, a3), (b, b1, b2, b2_low, b3)
    k, near, far, t_tube, t_plane, n0 = pl.pallas_call(
        functools.partial(tile_kernel, *sizes),
        out_shape=(
            shape(plane, NC * line),
            shape(rhs, line + rhs),
            shape(rhs, line + rhs),
            shape(rhs, NC * line),
            shape(rhs, plane),
            shape(rhs, rhs),
        ),
        in_specs=[SM] + [HBM] * 11,
        out_specs=[VM] * 6,
        scratch_shapes=[
            pltpu.VMEM((NC * line, 2 * half + PAD), BF16),
            pltpu.VMEM((plane, half + PAD), BF16),
            pltpu.VMEM((plane, half), BF16),
            pltpu.VMEM((plane, NC * line), F32),
            pltpu.SemaphoreType.DMA((4, NC + 5)),
        ],
        compiler_params=pltpu.CompilerParams(vmem_limit_bytes=60 * MIB),
        cost_estimate=pl.CostEstimate(
            flops=4 * plane * NC * line * 2 * half,
            bytes_accessed=2 * (plane + NC * line) * 2 * half,
            transcendentals=plane * NC * line,
        ),
        name="tile",
    )(at, tube, *a, *b)

    copies = small_kernel(
        functools.partial(share_kernel, NZ),
        shape(NZ, rhs, line + rhs),
        (near, other_core(far)),
        name="share",
    )
    sent, n0 = small_kernel(
        functools.partial(line_kernel, line),
        (shape(rhs, line + 2 * rhs), shape(rhs, rhs)),
        (exchange(copies, LINES), t_tube),
        name="line",
    )
    received = other_core(sent)
    copies = small_kernel(
        functools.partial(spread_kernel, rows, line),
        shape(NY * NX, rhs, rows + 2 * rhs),
        (at, sent, received),
        [SM, VM, VM],
        name="spread",
    )
    got = exchange(copies, PLANES)
    own = shape(rhs, rows)
    values = (at, got, n0, sent, received, t_tube, t_plane, k)
    near, far, d_own, weights, residual, rr1 = small_kernel(
        functools.partial(step_kernel, rows, rhs, line),
        (shape(rhs, line), shape(rhs, line + rhs), own, own, own, shape(rhs, rhs)),
        values,
        [SM] + [VM] * 7,
        limit=16,
        scratch=[pltpu.VMEM((rhs, plane), F32)],
        name="step",
    )
    return finish(rows, rhs, line, near, far, d_own, weights, residual, rr1)


def finish(rows, rhs, line, near, far, d_own, weights, residual, rr1):
    away = other_core(far)
    chunks = small_kernel(
        functools.partial(chunk_kernel, rows, line),
        shape(NZ, rhs, rows + rhs),
        (near, away, far),
        name="chunk",
    )
    own = shape(rhs, rows)
    image, copies = small_kernel(
        functools.partial(image_kernel, rows),
        (own, shape(NY * NX, rhs // 4, 4 * rhs)),
        (exchange(chunks, LINES), d_own),
        name="image",
    )
    weights, residual = small_kernel(
        functools.partial(last_kernel, rhs),
        (own, own),
        (exchange(copies, PLANES), rr1, d_own, image, weights, residual),
        name="last",
    )
    return weights.T, residual.T


def solution(mesh):
    in_specs = (P(AXES, None), P(AXES, None))
    out_specs = (P(AXES, None), P(AXES, None))
    return jax.shard_map(local, mesh=mesh, in_specs=in_specs, out_specs=out_specs, check_vma=False)
```

```python
import functools

import jax
import jax.numpy as jnp
from jax import lax
from jax.experimental import pallas as pl
from jax.experimental.pallas import tpu as pltpu
from jax.sharding import PartitionSpec as P

sharpness = 4.0
AXES = ("row", "col")
NZ, NY, NX, NC = 8, 4, 4, 2
HIGH = lax.Precision.HIGHEST
PAD = 128
MIB = 1024 * 1024
F32 = jnp.float32
BF16 = jnp.bfloat16
VM = pl.BlockSpec(memory_space=pltpu.VMEM)
SM = pl.BlockSpec(memory_space=pltpu.SMEM)
HBM = pl.BlockSpec(memory_space=pltpu.HBM)


def device(z, y, x, c):
    z, y, x = z % NZ, y % NY, x % NX
    return ((z * 2 + y % 2) * 2 + c) * 8 + (y // 2) * 4 + x


PLACES = [
    (z, y, x, c) for z in range(NZ) for y in range(NY) for x in range(NX) for c in range(NC)
]
LINES = [
    [device(z, y, x, c) for z in range(NZ)]
    for y in range(NY)
    for x in range(NX)
    for c in range(NC)
]
TUBES = [
    [device(z, y, x, c) for c in range(NC) for z in range(NZ)]
    for y in range(NY)
    for x in range(NX)
]
PLANES = [
    [device(z, y, x, c) for y in range(NY) for x in range(NX)]
    for z in range(NZ)
    for c in range(NC)
]


def from_x(value, k):
    return lax.ppermute(
        value, AXES, [(device(z, y, x + k, c), device(z, y, x, c)) for z, y, x, c in PLACES]
    )


def from_y(value, k):
    return lax.ppermute(
        value, AXES, [(device(z, y + k, x, c), device(z, y, x, c)) for z, y, x, c in PLACES]
    )


def other_core(value):
    return lax.ppermute(
        value, AXES, [(device(z, y, x, 1 - c), device(z, y, x, c)) for z, y, x, c in PLACES]
    )


def exchange(chunks, groups):
    return lax.all_to_all(chunks, AXES, 0, 0, axis_index_groups=groups, tiled=True)


def shape(*dims, dtype=F32):
    return jax.ShapeDtypeStruct(dims, dtype)


def mm(a, b):
    return jnp.dot(a, b, precision=HIGH, preferred_element_type=F32)


def nt(a, b):
    return lax.dot_general(
        a, b, (((1,), (1,)), ((), ())), precision=HIGH, preferred_element_type=F32
    )


def small_kernel(body, out, args, specs=None, limit=8, scratch=(), name=None):
    return pl.pallas_call(
        body,
        out_shape=out,
        in_specs=specs or [VM] * len(args),
        out_specs=jax.tree.map(lambda _: VM, out),
        scratch_shapes=list(scratch),
        compiler_params=pltpu.CompilerParams(vmem_limit_bytes=limit * MIB),
        name=name,
    )(*args)


def prepare_kernel(half, s_hbm, t_hbm, all_ref, first_ref, second_ref, s_ref, t_ref, sems):
    copies = [
        pltpu.make_async_copy(t_hbm, t_ref, sems.at[1]),
        pltpu.make_async_copy(s_hbm, s_ref, sems.at[0]),
    ]
    for copy in copies:
        copy.start()
    for copy in copies:
        copy.wait()
    sketches = s_ref[...]
    scale = jnp.sqrt(jnp.sum(sketches * sketches, axis=1, keepdims=True) + 1e-06)
    units = (sketches / scale).astype(BF16)
    targets = t_ref[...].T
    hi = targets.astype(BF16).astype(F32)
    mid = (targets - hi).astype(BF16).astype(F32)
    low = targets - hi - mid
    terms = jnp.concatenate([hi, mid, low, jnp.zeros_like(low)], axis=1).astype(BF16)
    all_ref[:, : 2 * half] = units
    all_ref[:, 2 * half :] = terms
    first_ref[:, :half] = units[:, :half]
    first_ref[:, half:] = terms
    second_ref[...] = units[:, half:]


def spans(rows):
    side = 4 * rows
    return [
        pl.ds(at, size)
        for at, size in (
            (0, side),
            (side, side),
            (2 * side, side // 2),
            (5 * side // 2, side // 2),
            (3 * side, side),
        )
    ]


def targets_of(terms, rhs):
    terms = terms.astype(F32).T
    return terms[:rhs] + terms[rhs : 2 * rhs] + terms[2 * rhs : 3 * rhs]


def tile_kernel(rows, rhs, half, at_ref, *refs):
    x_hbm, a_hbm, b_hbm = refs[0], refs[1:6], refs[6:11]
    k_ref, near_ref, far_ref, tx_ref, ty_ref, n0_ref = refs[11:17]
    x_ref, a_ref, b_ref, cos_ref, sems = refs[17:]
    line, quarter, last = 8 * rows, half // 2, half // 4
    dims = (((1,), (1,)), ((), ()))
    plans = (
        (0, quarter, a_hbm, a_ref, 0, quarter),
        (quarter, quarter, a_hbm, a_ref, quarter, quarter + PAD),
        (half, half - last, b_hbm, b_ref, 0, half - last),
        (2 * half - last, last + PAD, b_hbm, b_ref, half - last, last),
    )
    groups = []
    for i, (at_x, wide_x, pieces, ref, at_y, wide_y) in enumerate(plans):
        group = []
        of_x, of_y = pl.ds(at_x, wide_x), pl.ds(at_y, wide_y)
        for core in range(NC):
            of = pl.multiple_of(lax.rem(at_ref[3] + core, NC) * line, line)
            copy = pltpu.make_async_copy(
                x_hbm.at[pl.ds(of, line), of_x],
                x_ref.at[pl.ds(core * line, line), of_x],
                sems.at[i, core],
            )
            group.append(copy)
        for n, (to, piece) in enumerate(zip(spans(rows), pieces)):
            group.append(
                pltpu.make_async_copy(piece.at[:, of_y], ref.at[to, of_y], sems.at[i, NC + n])
            )
        groups.append(group)
        for copy in group:
            copy.start()
    for i, (at_x, wide_x, _, ref, at_y, wide_y) in enumerate(plans):
        for copy in groups[i]:
            copy.wait()
        wide = min(wide_x, wide_y)
        product = lax.dot_general(
            ref[:, at_y : at_y + wide],
            x_ref[:, at_x : at_x + wide],
            dims,
            preferred_element_type=F32,
        )
        to = k_ref if i < 2 else cos_ref
        if i % 2:
            to[...] += product
        else:
            to[...] = product
        if i == 1:
            ty = targets_of(a_ref[:, half:], rhs)
            ty_ref[...] = ty
            n0 = nt(ty, ty)
            n0_ref[...] = n0
            near_ref[:, line:] = n0
            far_ref[:, line:] = n0
    for y in range(4):
        for x in range(4):
            to, of = pl.ds((4 * y + x) * rows, rows), pl.ds((4 * x + y) * rows, rows)
            k_ref[to, :] = jnp.exp(sharpness * (k_ref[to, :] + cos_ref[of, :] - 1.0))
    tx_ref[...] = targets_of(x_ref[:, 2 * half :], rhs)
    product = mm(ty_ref[...], k_ref[...])
    near_ref[:, :line] = product[:, :line]
    far_ref[:, :line] = product[:, line:]


def share_kernel(count, a_ref, b_ref, out_ref):
    value = a_ref[...] + b_ref[...]
    for i in range(count):
        out_ref[i] = value


def line_kernel(line, part_ref, t_ref, send_ref, n0_ref):
    part = jnp.sum(part_ref[...], axis=0)
    rhs = part.shape[0]
    t = t_ref[:, :line]
    w = part[:, :line] - t
    n0_ref[...] = part[:, line:]
    send_ref[:, :line] = w
    send_ref[:, line : line + rhs] = nt(t, w)
    send_ref[:, line + rhs :] = nt(w, w)


def spread_kernel(rows, line, own_ref, near_ref, far_ref, out_ref):
    out_ref[0, :, :rows] = own_ref[...]
    out_ref[0, :, rows:] = near_ref[:, line:] + far_ref[:, line:]
    payload = out_ref[0]
    for i in range(1, NY * NX):
        out_ref[i] = payload


def eliminate(pairs):
    size = pairs[0][0].shape[0]
    row = lax.broadcasted_iota(jnp.int32, (size, size), 0)
    col = lax.broadcasted_iota(jnp.int32, (size, size), 1)
    pairs = list(pairs)
    block = 8
    for start in range(0, size, block):
        panels = [
            [
                jnp.broadcast_to(m[:, start + j : start + j + 1], (size, size))
                for j in range(block)
            ]
            for m, _ in pairs
        ]
        for j in range(block):
            k = start + j
            for n, (m, c) in enumerate(pairs):
                panel = panels[n]
                inverse = 1.0 / panel[j][k : k + 1, :]
                column = jnp.where(row == k, 0.0, panel[j])
                m_row, c_row = m[k : k + 1, :] * inverse, c[k : k + 1, :] * inverse
                pairs[n] = m - column * m_row, c - column * c_row
                for i in range(j + 1, block):
                    panel[i] = panel[i] - column * (panel[i][k : k + 1, :] * inverse)
    return [
        c / jnp.sum(jnp.where(row == col, m, 0.0), axis=1, keepdims=True) for m, c in pairs
    ]


def symmetric(matrix):
    return 0.5 * (matrix + matrix.T)


def step_kernel(rows, rhs, line, at_ref, *refs):
    got_ref, n0_ref, w_line, w_far, t_tube, t_plane, k_ref = refs[:7]
    out_ref, d_ref, weights_ref, residual_ref, rr_ref, w_ref, d_tube = refs[7:]
    got = jnp.sum(got_ref[...], axis=0)
    n0 = symmetric(n0_ref[...])
    n1, n2 = got[:, rows : rows + rhs], got[:, rows + rhs : rows + 2 * rhs]
    y, x = at_ref[1], at_ref[2]
    for dy in range(NY):
        for dx in range(NX):
            s = NX * dy + dx
            of = lax.rem(y + dy, NY) * NX + lax.rem(x + dx, NX)
            w_ref[:, s * rows : (s + 1) * rows] = got_ref[of][:, :rows]
    eye = (
        lax.broadcasted_iota(jnp.int32, (rhs, rhs), 0)
        == lax.broadcasted_iota(jnp.int32, (rhs, rhs), 1)
    ).astype(F32)
    a1, n0_inverse = eliminate([(symmetric(n1) + 2.0 * n0, n0), (n0, eye)])
    a1t = a1.T
    q = eye - 2.0 * a1
    qt = eye - 2.0 * a1t
    cross = mm(qt, mm(n1, a1))
    rr1 = mm(qt, mm(n0, q)) - cross - cross.T + mm(a1t, mm(n2, a1))
    mix = qt + mm(n0_inverse, rr1).T
    d_plane = mm(mix, t_plane[...]) - mm(a1t, w_ref[...])
    d_tube[:, :line] = mm(mix, t_tube[:, :line]) - mm(a1t, w_line[:, :line])
    d_tube[:, line:] = mm(mix, t_tube[:, line:]) - mm(a1t, w_far[:, :line])
    product = nt(d_tube[...], k_ref[...])
    d_own, t_own = d_plane[:, :rows], t_plane[:, :rows]
    gram = nt(d_plane, product) + nt(d_own, d_own)
    for dy in range(NY):
        for dx in range(NX):
            s = NX * dy + dx
            of = lax.rem(y + dy, NY) * NX + lax.rem(x + dx, NX)
            block = product[:, s * rows : (s + 1) * rows]
            out_ref[of] = jnp.concatenate([block, gram], axis=1)
    d_ref[...] = d_own
    weights_ref[...] = mm(a1t, t_own)
    residual_ref[...] = mm(qt, t_own) - mm(a1t, w_ref[:, :rows])
    rr_ref[...] = rr1


def image_kernel(rows, got_ref, d_ref, image_ref, out_ref):
    got = jnp.sum(got_ref[...], axis=0)
    image_ref[...] = got[:, :rows] + d_ref[...]
    gram = got[:, rows:]
    dense = jnp.concatenate([gram[8 * i : 8 * i + 8] for i in range(4)], axis=1)
    for i in range(NZ * NC):
        out_ref[i] = dense


def last_kernel(rhs, got_ref, rr, d_own, image, weights, residual, out_weights, out_residual):
    dense = jnp.sum(got_ref[...], axis=0)
    gram = jnp.concatenate([dense[:, rhs * i : rhs * (i + 1)] for i in range(4)], axis=0)
    (a2,) = eliminate([(symmetric(gram), rr[...])])
    a2t = a2.T
    out_weights[...] = weights[...] + mm(a2t, d_own[...])
    out_residual[...] = residual[...] - mm(a2t, image[...])


def local(sketches, targets):
    rows, rhs = targets.shape
    half = sketches.shape[1] // 2
    line, plane = NZ * rows, NY * NX * rows
    z = lax.axis_index("row") // 4
    y = lax.axis_index("row") // 2 % 2 + 2 * (lax.axis_index("col") // NX)
    x = lax.axis_index("col") % NX
    c = lax.axis_index("row") % NC
    at = jnp.stack([z, y, x, c]).astype(jnp.int32)
    sizes = (rows, rhs, half)

    units, first, second = small_kernel(
        functools.partial(prepare_kernel, half),
        (
            shape(rows, 2 * half + PAD, dtype=BF16),
            shape(rows, half + PAD, dtype=BF16),
            shape(rows, half, dtype=BF16),
        ),
        (sketches, targets.T),
        [HBM] * 2,
        limit=60,
        scratch=[
            pltpu.VMEM((rows, 2 * half), F32),
            pltpu.VMEM((rhs, rows), F32),
            pltpu.SemaphoreType.DMA((2,)),
        ],
        name="prepare",
    )
    tube = lax.all_gather(units, AXES, axis=0, tiled=True, axis_index_groups=TUBES)
    a = jnp.concatenate([first] + [from_x(first, k) for k in range(1, NX)], axis=0)
    b = jnp.concatenate([second] + [from_y(second, k) for k in range(1, NY)], axis=0)
    a, b = lax.optimization_barrier((a, b))
    a1, b1, a3, b3 = from_y(a, 1), from_x(b, 1), from_y(a, 3), from_x(b, 3)
    top = 2 * rows
    a2, b2 = from_y(a1[:top], 1), from_x(b1[:top], 1)
    a2_low, b2_low = from_y(a3[top:], 3), from_x(b3[top:], 3)
    a, b = (a, a1, a2, a2_low, a3), (b, b1, b2, b2_low, b3)
    k, near, far, t_tube, t_plane, n0 = pl.pallas_call(
        functools.partial(tile_kernel, *sizes),
        out_shape=(
            shape(plane, NC * line),
            shape(rhs, line + rhs),
            shape(rhs, line + rhs),
            shape(rhs, NC * line),
            shape(rhs, plane),
            shape(rhs, rhs),
        ),
        in_specs=[SM] + [HBM] * 11,
        out_specs=[VM] * 6,
        scratch_shapes=[
            pltpu.VMEM((NC * line, 2 * half + PAD), BF16),
            pltpu.VMEM((plane, half + PAD), BF16),
            pltpu.VMEM((plane, half), BF16),
            pltpu.VMEM((plane, NC * line), F32),
            pltpu.SemaphoreType.DMA((4, NC + 5)),
        ],
        compiler_params=pltpu.CompilerParams(vmem_limit_bytes=57 * MIB),
        cost_estimate=pl.CostEstimate(
            flops=4 * plane * NC * line * 2 * half,
            bytes_accessed=2 * (plane + NC * line) * 2 * half,
            transcendentals=plane * NC * line,
        ),
        name="tile",
    )(at, tube, *a, *b)

    copies = small_kernel(
        functools.partial(share_kernel, NZ),
        shape(NZ, rhs, line + rhs),
        (near, other_core(far)),
        name="share",
    )
    sent, n0 = small_kernel(
        functools.partial(line_kernel, line),
        (shape(rhs, line + 2 * rhs), shape(rhs, rhs)),
        (exchange(copies, LINES), t_tube),
        name="line",
    )
    w_own = lax.dynamic_slice(sent, (0, z * rows), (rhs, rows))
    received = other_core(sent)
    copies = small_kernel(
        functools.partial(spread_kernel, rows, line),
        shape(NY * NX, rhs, rows + 2 * rhs),
        (w_own, sent, received),
        name="spread",
    )
    got = exchange(copies, PLANES)
    own = shape(rhs, rows)
    values = (at, got, n0, sent, received, t_tube, t_plane, k)
    chunks, d_own, weights, residual, rr1 = small_kernel(
        functools.partial(step_kernel, rows, rhs, line),
        (shape(NY * NX, rhs, rows + rhs), own, own, own, shape(rhs, rhs)),
        values,
        [SM] + [VM] * 7,
        limit=16,
        scratch=[pltpu.VMEM((rhs, plane), F32), pltpu.VMEM((rhs, NC * line), F32)],
        name="step",
    )
    image, copies = small_kernel(
        functools.partial(image_kernel, rows),
        (own, shape(NZ * NC, rhs // 4, 4 * rhs)),
        (exchange(chunks, PLANES), d_own),
        name="image",
    )
    weights, residual = small_kernel(
        functools.partial(last_kernel, rhs),
        (own, own),
        (exchange(copies, TUBES), rr1, d_own, image, weights, residual),
        name="last",
    )
    return weights.T, residual.T


def solution(mesh):
    in_specs = (P(AXES, None), P(AXES, None))
    out_specs = (P(AXES, None), P(AXES, None))
    return jax.shard_map(local, mesh=mesh, in_specs=in_specs, out_specs=out_specs, check_vma=False)
```

```python
import functools

import jax
import jax.numpy as jnp
from jax import lax
from jax.experimental import pallas as pl
from jax.experimental.pallas import tpu as pltpu
from jax.sharding import PartitionSpec as P

sharpness = 4.0
AXES = ("row", "col")
NZ, NY, NX, NC = 8, 4, 4, 2
HIGH = lax.Precision.HIGHEST
PAD = 128
MIB = 1024 * 1024
F32 = jnp.float32
BF16 = jnp.bfloat16
VM = pl.BlockSpec(memory_space=pltpu.VMEM)
SM = pl.BlockSpec(memory_space=pltpu.SMEM)
HBM = pl.BlockSpec(memory_space=pltpu.HBM)


def device(z, y, x, c):
    z, y, x = z % NZ, y % NY, x % NX
    return ((z * 2 + y % 2) * 2 + c) * 8 + (y // 2) * 4 + x


PLACES = [
    (z, y, x, c) for z in range(NZ) for y in range(NY) for x in range(NX) for c in range(NC)
]
LINES = [
    [device(z, y, x, c) for z in range(NZ)]
    for y in range(NY)
    for x in range(NX)
    for c in range(NC)
]
TUBES = [
    [device(z, y, x, c) for c in range(NC) for z in range(NZ)]
    for y in range(NY)
    for x in range(NX)
]
PLANES = [
    [device(z, y, x, c) for y in range(NY) for x in range(NX)]
    for z in range(NZ)
    for c in range(NC)
]


def from_x(value, k):
    return lax.ppermute(
        value, AXES, [(device(z, y, x + k, c), device(z, y, x, c)) for z, y, x, c in PLACES]
    )


def from_y(value, k):
    return lax.ppermute(
        value, AXES, [(device(z, y + k, x, c), device(z, y, x, c)) for z, y, x, c in PLACES]
    )


def other_core(value):
    return lax.ppermute(
        value, AXES, [(device(z, y, x, 1 - c), device(z, y, x, c)) for z, y, x, c in PLACES]
    )


def exchange(chunks, groups):
    return lax.all_to_all(chunks, AXES, 0, 0, axis_index_groups=groups, tiled=True)


def shape(*dims, dtype=F32):
    return jax.ShapeDtypeStruct(dims, dtype)


def mm(a, b):
    return jnp.dot(a, b, precision=HIGH, preferred_element_type=F32)


def nt(a, b):
    return lax.dot_general(
        a, b, (((1,), (1,)), ((), ())), precision=HIGH, preferred_element_type=F32
    )


def small_kernel(body, out, args, specs=None, limit=8, scratch=(), name=None):
    return pl.pallas_call(
        body,
        out_shape=out,
        in_specs=specs or [VM] * len(args),
        out_specs=jax.tree.map(lambda _: VM, out),
        scratch_shapes=list(scratch),
        compiler_params=pltpu.CompilerParams(vmem_limit_bytes=limit * MIB),
        name=name,
    )(*args)


def prepare_kernel(half, s_hbm, t_hbm, all_ref, first_ref, second_ref, s_ref, t_ref, sems):
    copies = [
        pltpu.make_async_copy(t_hbm, t_ref, sems.at[1]),
        pltpu.make_async_copy(s_hbm, s_ref, sems.at[0]),
    ]
    for copy in copies:
        copy.start()
    for copy in copies:
        copy.wait()
    sketches = s_ref[...]
    scale = jnp.sqrt(jnp.sum(sketches * sketches, axis=1, keepdims=True) + 1e-06)
    units = (sketches / scale).astype(BF16)
    targets = t_ref[...].T
    hi = targets.astype(BF16).astype(F32)
    mid = (targets - hi).astype(BF16).astype(F32)
    low = targets - hi - mid
    terms = jnp.concatenate([hi, mid, low, jnp.zeros_like(low)], axis=1).astype(BF16)
    all_ref[:, : 2 * half] = units
    all_ref[:, 2 * half :] = terms
    first_ref[:, :half] = units[:, :half]
    first_ref[:, half:] = terms
    second_ref[...] = units[:, half:]


def spans(rows):
    side = 4 * rows
    return [
        pl.ds(at, size)
        for at, size in (
            (0, side),
            (side, side),
            (2 * side, side // 2),
            (5 * side // 2, side // 2),
            (3 * side, side),
        )
    ]


def targets_of(terms, rhs):
    terms = terms.astype(F32).T
    return terms[:rhs] + terms[rhs : 2 * rhs] + terms[2 * rhs : 3 * rhs]


def tile_kernel(rows, rhs, half, at_ref, *refs):
    x_hbm, a_hbm, b_hbm = refs[0], refs[1:6], refs[6:11]
    k_ref, near_ref, far_ref, tx_ref, ty_ref, n0_ref = refs[11:17]
    x_ref, a_ref, b_ref, cos_ref, sems = refs[17:]
    line, quarter, last = 8 * rows, half // 2, half // 4
    dims = (((1,), (1,)), ((), ()))
    plans = (
        (0, quarter, a_hbm, a_ref, 0, quarter),
        (quarter, quarter, a_hbm, a_ref, quarter, quarter + PAD),
        (half, half - last, b_hbm, b_ref, 0, half - last),
        (2 * half - last, last + PAD, b_hbm, b_ref, half - last, last),
    )
    groups = []
    for i, (at_x, wide_x, pieces, ref, at_y, wide_y) in enumerate(plans):
        group = []
        of_x, of_y = pl.ds(at_x, wide_x), pl.ds(at_y, wide_y)
        for core in range(NC):
            of = pl.multiple_of(lax.rem(at_ref[3] + core, NC) * line, line)
            copy = pltpu.make_async_copy(
                x_hbm.at[pl.ds(of, line), of_x],
                x_ref.at[pl.ds(core * line, line), of_x],
                sems.at[i, core],
            )
            group.append(copy)
        for n, (to, piece) in enumerate(zip(spans(rows), pieces)):
            group.append(
                pltpu.make_async_copy(piece.at[:, of_y], ref.at[to, of_y], sems.at[i, NC + n])
            )
        groups.append(group)
        for copy in group:
            copy.start()
    for i, (at_x, wide_x, _, ref, at_y, wide_y) in enumerate(plans):
        for copy in groups[i]:
            copy.wait()
        wide = min(wide_x, wide_y)
        product = lax.dot_general(
            ref[:, at_y : at_y + wide],
            x_ref[:, at_x : at_x + wide],
            dims,
            preferred_element_type=F32,
        )
        to = k_ref if i < 2 else cos_ref
        if i % 2:
            to[...] += product
        else:
            to[...] = product
        if i == 1:
            ty = targets_of(a_ref[:, half:], rhs)
            ty_ref[...] = ty
            n0 = nt(ty, ty)
            n0_ref[...] = n0
            near_ref[:rhs, line:] = n0
            far_ref[:, line:] = n0
    for y in range(4):
        for x in range(4):
            to, of = pl.ds((4 * y + x) * rows, rows), pl.ds((4 * x + y) * rows, rows)
            k_ref[to, :] = jnp.exp(sharpness * (k_ref[to, :] + cos_ref[of, :] - 1.0))
    tx = targets_of(x_ref[:, 2 * half :], rhs)
    tx_ref[...] = tx
    near_ref[rhs:, :line] = tx[:, :line]
    near_ref[rhs:, line:] = jnp.zeros((rhs, rhs), F32)
    product = mm(ty_ref[...], k_ref[...])
    near_ref[:rhs, :line] = product[:, :line]
    far_ref[:, :line] = product[:, line:]


def share_kernel(line, near_ref, far_ref, out_ref, t_ref):
    t_ref[...] = near_ref[far_ref.shape[0] :, :line]
    value = near_ref[: far_ref.shape[0]] + far_ref[...]
    rhs = value.shape[0]
    whole, half = line // 128 * 128, rhs // 2
    rest, gram = value[:, whole:line], value[:, line:]
    parts = [value[:, i : i + 128] for i in range(0, whole, 128)]
    parts.append(jnp.concatenate([rest[:half], rest[half:]], axis=1))
    parts.append(jnp.concatenate([gram[8 * i : 8 * i + 8] for i in range(4)], axis=1))
    at = 0
    for part in parts:
        out_ref[0, at : at + part.shape[0]] = part
        at += part.shape[0]
    dense = out_ref[0]
    for i in range(1, NZ):
        out_ref[i] = dense


def line_kernel(line, part_ref, t_ref, send_ref, n0_ref):
    dense = jnp.sum(part_ref[...], axis=0)
    rhs = send_ref.shape[0]
    whole, half = line // 128, rhs // 2
    parts = [dense[rhs * i : rhs * (i + 1)] for i in range(whole)]
    rest, gram = dense[rhs * whole : rhs * whole + half], dense[rhs * whole + half :]
    parts.append(jnp.concatenate([rest[:, :64], rest[:, 64:]], axis=0))
    t = t_ref[...]
    w = jnp.concatenate(parts, axis=1) - t
    n0_ref[...] = jnp.concatenate([gram[:, rhs * i : rhs * (i + 1)] for i in range(4)], axis=0)
    send_ref[:, :line] = w
    send_ref[:, line : line + rhs] = nt(t, w)
    send_ref[:, line + rhs :] = nt(w, w)


def spread_kernel(rows, line, own_ref, near_ref, far_ref, out_ref):
    out_ref[0, :, :rows] = own_ref[...]
    out_ref[0, :, rows:] = near_ref[:, line:] + far_ref[:, line:]
    payload = out_ref[0]
    for i in range(1, NY * NX):
        out_ref[i] = payload


def eliminate(pairs):
    size = pairs[0][0].shape[0]
    row = lax.broadcasted_iota(jnp.int32, (size, size), 0)
    col = lax.broadcasted_iota(jnp.int32, (size, size), 1)
    pairs = list(pairs)
    block = 8
    for start in range(0, size, block):
        panels = [
            [
                jnp.broadcast_to(m[:, start + j : start + j + 1], (size, size))
                for j in range(block)
            ]
            for m, _ in pairs
        ]
        for j in range(block):
            k = start + j
            for n, (m, c) in enumerate(pairs):
                panel = panels[n]
                inverse = 1.0 / panel[j][k : k + 1, :]
                column = jnp.where(row == k, 0.0, panel[j])
                m_row, c_row = m[k : k + 1, :] * inverse, c[k : k + 1, :] * inverse
                pairs[n] = m - column * m_row, c - column * c_row
                for i in range(j + 1, block):
                    panel[i] = panel[i] - column * (panel[i][k : k + 1, :] * inverse)
    return [
        c / jnp.sum(jnp.where(row == col, m, 0.0), axis=1, keepdims=True) for m, c in pairs
    ]


def symmetric(matrix):
    return 0.5 * (matrix + matrix.T)


def step_kernel(rows, rhs, line, at_ref, *refs):
    got_ref, n0_ref, w_line, w_far, t_tube, t_plane, k_ref = refs[:7]
    out_ref, d_ref, weights_ref, residual_ref, rr_ref, w_ref, d_tube = refs[7:]
    got = jnp.sum(got_ref[...], axis=0)
    n0 = symmetric(n0_ref[...])
    n1, n2 = got[:, rows : rows + rhs], got[:, rows + rhs : rows + 2 * rhs]
    y, x = at_ref[1], at_ref[2]
    for dy in range(NY):
        for dx in range(NX):
            s = NX * dy + dx
            of = lax.rem(y + dy, NY) * NX + lax.rem(x + dx, NX)
            w_ref[:, s * rows : (s + 1) * rows] = got_ref[of][:, :rows]
    eye = (
        lax.broadcasted_iota(jnp.int32, (rhs, rhs), 0)
        == lax.broadcasted_iota(jnp.int32, (rhs, rhs), 1)
    ).astype(F32)
    a1, n0_inverse = eliminate([(symmetric(n1) + 2.0 * n0, n0), (n0, eye)])
    a1t = a1.T
    q = eye - 2.0 * a1
    qt = eye - 2.0 * a1t
    cross = mm(qt, mm(n1, a1))
    rr1 = mm(qt, mm(n0, q)) - cross - cross.T + mm(a1t, mm(n2, a1))
    mix = qt + mm(n0_inverse, rr1).T
    d_plane = mm(mix, t_plane[...]) - mm(a1t, w_ref[...])
    d_tube[:, :line] = mm(mix, t_tube[:, :line]) - mm(a1t, w_line[:, :line])
    d_tube[:, line:] = mm(mix, t_tube[:, line:]) - mm(a1t, w_far[:, :line])
    product = nt(d_tube[...], k_ref[...])
    d_own, t_own = d_plane[:, :rows], t_plane[:, :rows]
    gram = nt(d_plane, product) + nt(d_own, d_own)
    for dy in range(NY):
        for dx in range(NX):
            s = NX * dy + dx
            of = lax.rem(y + dy, NY) * NX + lax.rem(x + dx, NX)
            block = product[:, s * rows : (s + 1) * rows]
            out_ref[of] = jnp.concatenate([block, gram], axis=1)
    d_ref[...] = d_own
    weights_ref[...] = mm(a1t, t_own)
    residual_ref[...] = mm(qt, t_own) - mm(a1t, w_ref[:, :rows])
    rr_ref[...] = rr1


def image_kernel(rows, got_ref, d_ref, image_ref, out_ref):
    got = jnp.sum(got_ref[...], axis=0)
    image_ref[...] = got[:, :rows] + d_ref[...]
    gram = got[:, rows:]
    dense = jnp.concatenate([gram[8 * i : 8 * i + 8] for i in range(4)], axis=1)
    for i in range(NZ * NC):
        out_ref[i] = dense


def last_kernel(rhs, got_ref, rr, d_own, image, weights, residual, out_weights, out_residual):
    dense = jnp.sum(got_ref[...], axis=0)
    gram = jnp.concatenate([dense[:, rhs * i : rhs * (i + 1)] for i in range(4)], axis=0)
    (a2,) = eliminate([(symmetric(gram), rr[...])])
    a2t = a2.T
    out_weights[...] = weights[...] + mm(a2t, d_own[...])
    out_residual[...] = residual[...] - mm(a2t, image[...])


def local(sketches, targets):
    rows, rhs = targets.shape
    half = sketches.shape[1] // 2
    line, plane = NZ * rows, NY * NX * rows
    z = lax.axis_index("row") // 4
    y = lax.axis_index("row") // 2 % 2 + 2 * (lax.axis_index("col") // NX)
    x = lax.axis_index("col") % NX
    c = lax.axis_index("row") % NC
    at = jnp.stack([z, y, x, c]).astype(jnp.int32)
    sizes = (rows, rhs, half)

    units, first, second = small_kernel(
        functools.partial(prepare_kernel, half),
        (
            shape(rows, 2 * half + PAD, dtype=BF16),
            shape(rows, half + PAD, dtype=BF16),
            shape(rows, half, dtype=BF16),
        ),
        (sketches, targets.T),
        [HBM] * 2,
        limit=60,
        scratch=[
            pltpu.VMEM((rows, 2 * half), F32),
            pltpu.VMEM((rhs, rows), F32),
            pltpu.SemaphoreType.DMA((2,)),
        ],
        name="prepare",
    )
    tube = lax.all_gather(units, AXES, axis=0, tiled=True, axis_index_groups=TUBES)
    a = jnp.concatenate([first] + [from_x(first, k) for k in range(1, NX)], axis=0)
    b = jnp.concatenate([second] + [from_y(second, k) for k in range(1, NY)], axis=0)
    a, b = lax.optimization_barrier((a, b))
    a1, b1, a3, b3 = from_y(a, 1), from_x(b, 1), from_y(a, 3), from_x(b, 3)
    top = 2 * rows
    a2, b2 = from_y(a1[:top], 1), from_x(b1[:top], 1)
    a2_low, b2_low = from_y(a3[top:], 3), from_x(b3[top:], 3)
    a, b = (a, a1, a2, a2_low, a3), (b, b1, b2, b2_low, b3)
    k, near, far, t_tube, t_plane, n0 = pl.pallas_call(
        functools.partial(tile_kernel, *sizes),
        out_shape=(
            shape(plane, NC * line),
            shape(2 * rhs, line + rhs),
            shape(rhs, line + rhs),
            shape(rhs, NC * line),
            shape(rhs, plane),
            shape(rhs, rhs),
        ),
        in_specs=[SM] + [HBM] * 11,
        out_specs=[VM] * 6,
        scratch_shapes=[
            pltpu.VMEM((NC * line, 2 * half + PAD), BF16),
            pltpu.VMEM((plane, half + PAD), BF16),
            pltpu.VMEM((plane, half), BF16),
            pltpu.VMEM((plane, NC * line), F32),
            pltpu.SemaphoreType.DMA((4, NC + 5)),
        ],
        compiler_params=pltpu.CompilerParams(vmem_limit_bytes=52 * MIB),
        cost_estimate=pl.CostEstimate(
            flops=4 * plane * NC * line * 2 * half,
            bytes_accessed=2 * (plane + NC * line) * 2 * half,
            transcendentals=plane * NC * line,
        ),
        name="tile",
    )(at, tube, *a, *b)

    copies, t_line = small_kernel(
        functools.partial(share_kernel, line),
        (shape(NZ, rhs * (line + rhs) // 128, 128), shape(rhs, line)),
        (near, other_core(far)),
        name="share",
    )
    sent, n0 = small_kernel(
        functools.partial(line_kernel, line),
        (shape(rhs, line + 2 * rhs), shape(rhs, rhs)),
        (exchange(copies, LINES), t_line),
        name="line",
    )
    w_own = lax.dynamic_slice(sent, (0, z * rows), (rhs, rows))
    received = other_core(sent)
    copies = small_kernel(
        functools.partial(spread_kernel, rows, line),
        shape(NY * NX, rhs, rows + 2 * rhs),
        (w_own, sent, received),
        name="spread",
    )
    got = exchange(copies, PLANES)
    own = shape(rhs, rows)
    values = (at, got, n0, sent, received, t_tube, t_plane, k)
    chunks, d_own, weights, residual, rr1 = small_kernel(
        functools.partial(step_kernel, rows, rhs, line),
        (shape(NY * NX, rhs, rows + rhs), own, own, own, shape(rhs, rhs)),
        values,
        [SM] + [VM] * 7,
        limit=16,
        scratch=[pltpu.VMEM((rhs, plane), F32), pltpu.VMEM((rhs, NC * line), F32)],
        name="step",
    )
    image, copies = small_kernel(
        functools.partial(image_kernel, rows),
        (own, shape(NZ * NC, rhs // 4, 4 * rhs)),
        (exchange(chunks, PLANES), d_own),
        name="image",
    )
    weights, residual = small_kernel(
        functools.partial(last_kernel, rhs),
        (own, own),
        (exchange(copies, TUBES), rr1, d_own, image, weights, residual),
        name="last",
    )
    return weights.T, residual.T


def solution(mesh):
    in_specs = (P(AXES, None), P(AXES, None))
    out_specs = (P(AXES, None), P(AXES, None))
    return jax.shard_map(local, mesh=mesh, in_specs=in_specs, out_specs=out_specs, check_vma=False)
```

```python
import functools

import jax
import jax.numpy as jnp
from jax import lax
from jax.experimental import pallas as pl
from jax.experimental.pallas import tpu as pltpu
from jax.sharding import PartitionSpec as P

sharpness = 4.0
AXES = ("row", "col")
NZ, NY, NX, NC = 8, 4, 4, 2
HIGH = lax.Precision.HIGHEST
PAD = 128
MIB = 1024 * 1024
F32 = jnp.float32
BF16 = jnp.bfloat16
VM = pl.BlockSpec(memory_space=pltpu.VMEM)
SM = pl.BlockSpec(memory_space=pltpu.SMEM)
HBM = pl.BlockSpec(memory_space=pltpu.HBM)


def device(z, y, x, c):
    z, y, x = z % NZ, y % NY, x % NX
    return ((z * 2 + y % 2) * 2 + c) * 8 + (y // 2) * 4 + x


PLACES = [
    (z, y, x, c) for z in range(NZ) for y in range(NY) for x in range(NX) for c in range(NC)
]
LINES = [
    [device(z + 2 * c, y, x, c) for z in (0, 4, 1, 5, 2, 6, 3, 7)]
    for y in range(NY)
    for x in range(NX)
    for c in range(NC)
]
TUBES = [
    [device(z, y, x, c) for c in range(NC) for z in range(NZ)]
    for y in range(NY)
    for x in range(NX)
]
PLANES = [
    [device(z, y, x, c) for y in range(NY) for x in range(NX)]
    for z in range(NZ)
    for c in range(NC)
]


def from_x(value, k):
    return lax.ppermute(
        value, AXES, [(device(z, y, x + k, c), device(z, y, x, c)) for z, y, x, c in PLACES]
    )


def from_y(value, k):
    return lax.ppermute(
        value, AXES, [(device(z, y + k, x, c), device(z, y, x, c)) for z, y, x, c in PLACES]
    )


def other_core(value):
    return lax.ppermute(
        value, AXES, [(device(z, y, x, 1 - c), device(z, y, x, c)) for z, y, x, c in PLACES]
    )


def exchange(chunks, groups):
    return lax.all_to_all(chunks, AXES, 0, 0, axis_index_groups=groups, tiled=True)


def shape(*dims, dtype=F32):
    return jax.ShapeDtypeStruct(dims, dtype)


def mm(a, b):
    return jnp.dot(a, b, precision=HIGH, preferred_element_type=F32)


def nt(a, b):
    return lax.dot_general(
        a, b, (((1,), (1,)), ((), ())), precision=HIGH, preferred_element_type=F32
    )


def small_kernel(body, out, args, specs=None, limit=8, scratch=(), name=None):
    return pl.pallas_call(
        body,
        out_shape=out,
        in_specs=specs or [VM] * len(args),
        out_specs=jax.tree.map(lambda _: VM, out),
        scratch_shapes=list(scratch),
        compiler_params=pltpu.CompilerParams(vmem_limit_bytes=limit * MIB),
        name=name,
    )(*args)


def prepare_kernel(half, s_hbm, t_hbm, all_ref, first_ref, second_ref, s_ref, t_ref, sems):
    copies = [
        pltpu.make_async_copy(t_hbm, t_ref, sems.at[1]),
        pltpu.make_async_copy(s_hbm, s_ref, sems.at[0]),
    ]
    for copy in copies:
        copy.start()
    for copy in copies:
        copy.wait()
    sketches = s_ref[...]
    scale = jnp.sqrt(jnp.sum(sketches * sketches, axis=1, keepdims=True) + 1e-06)
    units = (sketches / scale).astype(BF16)
    targets = t_ref[...].T
    hi = targets.astype(BF16).astype(F32)
    mid = (targets - hi).astype(BF16).astype(F32)
    low = targets - hi - mid
    terms = jnp.concatenate([hi, mid, low, jnp.zeros_like(low)], axis=1).astype(BF16)
    all_ref[:, : 2 * half] = units
    all_ref[:, 2 * half :] = terms
    first_ref[:, :half] = units[:, :half]
    first_ref[:, half:] = terms
    second_ref[...] = units[:, half:]


def spans(rows):
    side = 4 * rows
    return [
        pl.ds(at, size)
        for at, size in (
            (0, side),
            (side, side),
            (2 * side, side // 2),
            (5 * side // 2, side // 2),
            (3 * side, side),
        )
    ]


def targets_of(terms, rhs):
    terms = terms.astype(F32).T
    return terms[:rhs] + terms[rhs : 2 * rhs] + terms[2 * rhs : 3 * rhs]


def tile_kernel(rows, rhs, half, at_ref, *refs):
    x_hbm, a_hbm, b_hbm = refs[0], refs[1:6], refs[6:11]
    k_ref, near_ref, far_ref, tx_ref, ty_ref, n0_ref = refs[11:17]
    x_ref, a_ref, b_ref, cos_ref, sems = refs[17:]
    line, quarter, last = 8 * rows, half // 2, half // 4
    dims = (((1,), (1,)), ((), ()))
    plans = (
        (0, quarter, a_hbm, a_ref, 0, quarter),
        (quarter, quarter, a_hbm, a_ref, quarter, quarter + PAD),
        (half, half - last, b_hbm, b_ref, 0, half - last),
        (2 * half - last, last + PAD, b_hbm, b_ref, half - last, last),
    )
    groups = []
    for i, (at_x, wide_x, pieces, ref, at_y, wide_y) in enumerate(plans):
        group = []
        of_x, of_y = pl.ds(at_x, wide_x), pl.ds(at_y, wide_y)
        for core in range(NC):
            of = pl.multiple_of(lax.rem(at_ref[3] + core, NC) * line, line)
            copy = pltpu.make_async_copy(
                x_hbm.at[pl.ds(of, line), of_x],
                x_ref.at[pl.ds(core * line, line), of_x],
                sems.at[i, core],
            )
            group.append(copy)
        for n, (to, piece) in enumerate(zip(spans(rows), pieces)):
            group.append(
                pltpu.make_async_copy(piece.at[:, of_y], ref.at[to, of_y], sems.at[i, NC + n])
            )
        groups.append(group)
        for copy in group:
            copy.start()
    for i, (at_x, wide_x, _, ref, at_y, wide_y) in enumerate(plans):
        for copy in groups[i]:
            copy.wait()
        wide = min(wide_x, wide_y)
        product = lax.dot_general(
            ref[:, at_y : at_y + wide],
            x_ref[:, at_x : at_x + wide],
            dims,
            preferred_element_type=F32,
        )
        to = k_ref if i < 2 else cos_ref
        if i % 2:
            to[...] += product
        else:
            to[...] = product
        if i == 1:
            ty = targets_of(a_ref[:, half:], rhs)
            ty_ref[...] = ty
            n0 = nt(ty, ty)
            n0_ref[...] = n0
            near_ref[:rhs, line:] = n0
            far_ref[:, line:] = n0
    for y in range(4):
        for x in range(4):
            to, of = pl.ds((4 * y + x) * rows, rows), pl.ds((4 * x + y) * rows, rows)
            k_ref[to, :] = jnp.exp(sharpness * (k_ref[to, :] + cos_ref[of, :] - 1.0))
    tx = targets_of(x_ref[:, 2 * half :], rhs)
    tx_ref[...] = tx
    near_ref[rhs:, :line] = tx[:, :line]
    near_ref[rhs:, line:] = jnp.zeros((rhs, rhs), F32)
    product = mm(ty_ref[...], k_ref[...])
    near_ref[:rhs, :line] = product[:, :line]
    far_ref[:, :line] = product[:, line:]


def share_kernel(line, near_ref, far_ref, out_ref, t_ref):
    t_ref[...] = near_ref[far_ref.shape[0] :, :line]
    value = near_ref[: far_ref.shape[0]] + far_ref[...]
    rhs = value.shape[0]
    whole, half = line // 128 * 128, rhs // 2
    rest, gram = value[:, whole:line], value[:, line:]
    parts = [value[:, i : i + 128] for i in range(0, whole, 128)]
    parts.append(jnp.concatenate([rest[:half], rest[half:]], axis=1))
    parts.append(jnp.concatenate([gram[8 * i : 8 * i + 8] for i in range(4)], axis=1))
    at = 0
    for part in parts:
        out_ref[0, at : at + part.shape[0]] = part
        at += part.shape[0]
    dense = out_ref[0]
    for i in range(1, NZ):
        out_ref[i] = dense


def line_kernel(line, part_ref, t_ref, send_ref, n0_ref):
    dense = jnp.sum(part_ref[...], axis=0)
    rhs = send_ref.shape[0]
    whole, half = line // 128, rhs // 2
    parts = [dense[rhs * i : rhs * (i + 1)] for i in range(whole)]
    rest, gram = dense[rhs * whole : rhs * whole + half], dense[rhs * whole + half :]
    parts.append(jnp.concatenate([rest[:, :64], rest[:, 64:]], axis=0))
    t = t_ref[...]
    w = jnp.concatenate(parts, axis=1) - t
    n0_ref[...] = jnp.concatenate([gram[:, rhs * i : rhs * (i + 1)] for i in range(4)], axis=0)
    send_ref[:, :line] = w
    send_ref[:, line : line + rhs] = nt(t, w)
    send_ref[:, line + rhs :] = nt(w, w)


def spread_kernel(rows, line, own_ref, near_ref, far_ref, out_ref):
    out_ref[0, :, :rows] = own_ref[...]
    out_ref[0, :, rows:] = near_ref[:, line:] + far_ref[:, line:]
    payload = out_ref[0]
    for i in range(1, NY * NX):
        out_ref[i] = payload


def eliminate(pairs):
    size = pairs[0][0].shape[0]
    row = lax.broadcasted_iota(jnp.int32, (size, size), 0)
    col = lax.broadcasted_iota(jnp.int32, (size, size), 1)
    pairs = list(pairs)
    block = 8
    for start in range(0, size, block):
        panels = [
            [
                jnp.broadcast_to(m[:, start + j : start + j + 1], (size, size))
                for j in range(block)
            ]
            for m, _ in pairs
        ]
        for j in range(block):
            k = start + j
            for n, (m, c) in enumerate(pairs):
                panel = panels[n]
                inverse = 1.0 / panel[j][k : k + 1, :]
                column = jnp.where(row == k, 0.0, panel[j])
                m_row, c_row = m[k : k + 1, :] * inverse, c[k : k + 1, :] * inverse
                pairs[n] = m - column * m_row, c - column * c_row
                for i in range(j + 1, block):
                    panel[i] = panel[i] - column * (panel[i][k : k + 1, :] * inverse)
    return [
        c / jnp.sum(jnp.where(row == col, m, 0.0), axis=1, keepdims=True) for m, c in pairs
    ]


def symmetric(matrix):
    return 0.5 * (matrix + matrix.T)


def step_kernel(rows, rhs, line, at_ref, *refs):
    got_ref, n0_ref, w_line, w_far, t_tube, t_plane, k_ref = refs[:7]
    out_ref, d_ref, weights_ref, residual_ref, rr_ref, w_ref, d_tube = refs[7:]
    got = jnp.sum(got_ref[...], axis=0)
    n0 = symmetric(n0_ref[...])
    n1, n2 = got[:, rows : rows + rhs], got[:, rows + rhs : rows + 2 * rhs]
    y, x = at_ref[1], at_ref[2]
    for dy in range(NY):
        for dx in range(NX):
            s = NX * dy + dx
            of = lax.rem(y + dy, NY) * NX + lax.rem(x + dx, NX)
            w_ref[:, s * rows : (s + 1) * rows] = got_ref[of][:, :rows]
    eye = (
        lax.broadcasted_iota(jnp.int32, (rhs, rhs), 0)
        == lax.broadcasted_iota(jnp.int32, (rhs, rhs), 1)
    ).astype(F32)
    a1, n0_inverse = eliminate([(symmetric(n1) + 2.0 * n0, n0), (n0, eye)])
    a1t = a1.T
    q = eye - 2.0 * a1
    qt = eye - 2.0 * a1t
    cross = mm(qt, mm(n1, a1))
    rr1 = mm(qt, mm(n0, q)) - cross - cross.T + mm(a1t, mm(n2, a1))
    mix = qt + mm(n0_inverse, rr1).T
    d_plane = mm(mix, t_plane[...]) - mm(a1t, w_ref[...])
    d_tube[:, :line] = mm(mix, t_tube[:, :line]) - mm(a1t, w_line[:, :line])
    d_tube[:, line:] = mm(mix, t_tube[:, line:]) - mm(a1t, w_far[:, :line])
    product = nt(d_tube[...], k_ref[...])
    d_own, t_own = d_plane[:, :rows], t_plane[:, :rows]
    gram = nt(d_plane, product) + nt(d_own, d_own)
    for dy in range(NY):
        for dx in range(NX):
            s = NX * dy + dx
            of = lax.rem(y + dy, NY) * NX + lax.rem(x + dx, NX)
            block = product[:, s * rows : (s + 1) * rows]
            out_ref[of] = jnp.concatenate([block, gram], axis=1)
    d_ref[...] = d_own
    weights_ref[...] = mm(a1t, t_own)
    residual_ref[...] = mm(qt, t_own) - mm(a1t, w_ref[:, :rows])
    rr_ref[...] = rr1


def image_kernel(rows, got_ref, d_ref, image_ref, out_ref):
    got = jnp.sum(got_ref[...], axis=0)
    image_ref[...] = got[:, :rows] + d_ref[...]
    gram = got[:, rows:]
    dense = jnp.concatenate([gram[8 * i : 8 * i + 8] for i in range(4)], axis=1)
    for i in range(NZ * NC):
        out_ref[i] = dense


def last_kernel(rhs, got_ref, rr, d_own, image, weights, residual, out_weights, out_residual):
    dense = jnp.sum(got_ref[...], axis=0)
    gram = jnp.concatenate([dense[:, rhs * i : rhs * (i + 1)] for i in range(4)], axis=0)
    (a2,) = eliminate([(symmetric(gram), rr[...])])
    a2t = a2.T
    out_weights[...] = weights[...] + mm(a2t, d_own[...])
    out_residual[...] = residual[...] - mm(a2t, image[...])


def local(sketches, targets):
    rows, rhs = targets.shape
    half = sketches.shape[1] // 2
    line, plane = NZ * rows, NY * NX * rows
    z = lax.axis_index("row") // 4
    y = lax.axis_index("row") // 2 % 2 + 2 * (lax.axis_index("col") // NX)
    x = lax.axis_index("col") % NX
    c = lax.axis_index("row") % NC
    at = jnp.stack([z, y, x, c]).astype(jnp.int32)
    sizes = (rows, rhs, half)

    units, first, second = small_kernel(
        functools.partial(prepare_kernel, half),
        (
            shape(rows, 2 * half + PAD, dtype=BF16),
            shape(rows, half + PAD, dtype=BF16),
            shape(rows, half, dtype=BF16),
        ),
        (sketches, targets.T),
        [HBM] * 2,
        limit=60,
        scratch=[
            pltpu.VMEM((rows, 2 * half), F32),
            pltpu.VMEM((rhs, rows), F32),
            pltpu.SemaphoreType.DMA((2,)),
        ],
        name="prepare",
    )
    tube = lax.all_gather(units, AXES, axis=0, tiled=True, axis_index_groups=TUBES)
    a = jnp.concatenate([first] + [from_x(first, k) for k in range(1, NX)], axis=0)
    b = jnp.concatenate([second] + [from_y(second, k) for k in range(1, NY)], axis=0)
    a, b = lax.optimization_barrier((a, b))
    a1, b1, a3, b3 = from_y(a, 1), from_x(b, 1), from_y(a, 3), from_x(b, 3)
    top = 2 * rows
    a2, b2 = from_y(a1[:top], 1), from_x(b1[:top], 1)
    a2_low, b2_low = from_y(a3[top:], 3), from_x(b3[top:], 3)
    a, b = (a, a1, a2, a2_low, a3), (b, b1, b2, b2_low, b3)
    k, near, far, t_tube, t_plane, n0 = pl.pallas_call(
        functools.partial(tile_kernel, *sizes),
        out_shape=(
            shape(plane, NC * line),
            shape(2 * rhs, line + rhs),
            shape(rhs, line + rhs),
            shape(rhs, NC * line),
            shape(rhs, plane),
            shape(rhs, rhs),
        ),
        in_specs=[SM] + [HBM] * 11,
        out_specs=[VM] * 6,
        scratch_shapes=[
            pltpu.VMEM((NC * line, 2 * half + PAD), BF16),
            pltpu.VMEM((plane, half + PAD), BF16),
            pltpu.VMEM((plane, half), BF16),
            pltpu.VMEM((plane, NC * line), F32),
            pltpu.SemaphoreType.DMA((4, NC + 5)),
        ],
        compiler_params=pltpu.CompilerParams(vmem_limit_bytes=52 * MIB),
        cost_estimate=pl.CostEstimate(
            flops=4 * plane * NC * line * 2 * half,
            bytes_accessed=2 * (plane + NC * line) * 2 * half,
            transcendentals=plane * NC * line,
        ),
        name="tile",
    )(at, tube, *a, *b)

    copies, t_line = small_kernel(
        functools.partial(share_kernel, line),
        (shape(NZ, rhs * (line + rhs) // 128, 128), shape(rhs, line)),
        (near, other_core(far)),
        name="share",
    )
    sent, n0 = small_kernel(
        functools.partial(line_kernel, line),
        (shape(rhs, line + 2 * rhs), shape(rhs, rhs)),
        (exchange(copies, LINES), t_line),
        name="line",
    )
    w_own = lax.dynamic_slice(sent, (0, z * rows), (rhs, rows))
    received = other_core(sent)
    copies = small_kernel(
        functools.partial(spread_kernel, rows, line),
        shape(NY * NX, rhs, rows + 2 * rhs),
        (w_own, sent, received),
        name="spread",
    )
    got = exchange(copies, PLANES)
    own = shape(rhs, rows)
    values = (at, got, n0, sent, received, t_tube, t_plane, k)
    chunks, d_own, weights, residual, rr1 = small_kernel(
        functools.partial(step_kernel, rows, rhs, line),
        (shape(NY * NX, rhs, rows + rhs), own, own, own, shape(rhs, rhs)),
        values,
        [SM] + [VM] * 7,
        limit=16,
        scratch=[pltpu.VMEM((rhs, plane), F32), pltpu.VMEM((rhs, NC * line), F32)],
        name="step",
    )
    image, copies = small_kernel(
        functools.partial(image_kernel, rows),
        (own, shape(NZ * NC, rhs // 4, 4 * rhs)),
        (exchange(chunks, PLANES), d_own),
        name="image",
    )
    weights, residual = small_kernel(
        functools.partial(last_kernel, rhs),
        (own, own),
        (exchange(copies, TUBES), rr1, d_own, image, weights, residual),
        name="last",
    )
    return weights.T, residual.T


def solution(mesh):
    in_specs = (P(AXES, None), P(AXES, None))
    out_specs = (P(AXES, None), P(AXES, None))
    return jax.shard_map(local, mesh=mesh, in_specs=in_specs, out_specs=out_specs, check_vma=False)
```

```python
import functools

import jax
import jax.numpy as jnp
from jax import lax
from jax.experimental import pallas as pl
from jax.experimental.pallas import tpu as pltpu
from jax.sharding import PartitionSpec as P

sharpness = 4.0
AXES = ("row", "col")
NZ, NY, NX, NC = 8, 4, 4, 2
HIGH = lax.Precision.HIGHEST
PAD = 128
MIB = 1024 * 1024
F32 = jnp.float32
BF16 = jnp.bfloat16
VM = pl.BlockSpec(memory_space=pltpu.VMEM)
SM = pl.BlockSpec(memory_space=pltpu.SMEM)
HBM = pl.BlockSpec(memory_space=pltpu.HBM)


def device(z, y, x, c):
    z, y, x = z % NZ, y % NY, x % NX
    return ((z * 2 + y % 2) * 2 + c) * 8 + (y // 2) * 4 + x


PLACES = [
    (z, y, x, c) for z in range(NZ) for y in range(NY) for x in range(NX) for c in range(NC)
]
LINES = [
    [device(z, y, x, c) for z in (0, 4, 1, 5, 2, 6, 3, 7)]
    for y in range(NY)
    for x in range(NX)
    for c in range(NC)
]
TUBES = [
    [device(z, y, x, c) for c in range(NC) for z in range(NZ)]
    for y in range(NY)
    for x in range(NX)
]
PLANES = [
    [device(z, y, x, c) for y in range(NY) for x in range(NX)]
    for z in range(NZ)
    for c in range(NC)
]


def from_x(value, k):
    return lax.ppermute(
        value, AXES, [(device(z, y, x + k, c), device(z, y, x, c)) for z, y, x, c in PLACES]
    )


def from_y(value, k):
    return lax.ppermute(
        value, AXES, [(device(z, y + k, x, c), device(z, y, x, c)) for z, y, x, c in PLACES]
    )


def other_core(value):
    return lax.ppermute(
        value, AXES, [(device(z, y, x, 1 - c), device(z, y, x, c)) for z, y, x, c in PLACES]
    )


def exchange(chunks, groups):
    return lax.all_to_all(chunks, AXES, 0, 0, axis_index_groups=groups, tiled=True)


def shape(*dims, dtype=F32):
    return jax.ShapeDtypeStruct(dims, dtype)


def mm(a, b):
    return jnp.dot(a, b, precision=HIGH, preferred_element_type=F32)


def nt(a, b):
    return lax.dot_general(
        a, b, (((1,), (1,)), ((), ())), precision=HIGH, preferred_element_type=F32
    )


def small_kernel(body, out, args, specs=None, limit=8, scratch=(), name=None):
    return pl.pallas_call(
        body,
        out_shape=out,
        in_specs=specs or [VM] * len(args),
        out_specs=jax.tree.map(lambda _: VM, out),
        scratch_shapes=list(scratch),
        compiler_params=pltpu.CompilerParams(vmem_limit_bytes=limit * MIB),
        name=name,
    )(*args)


def prepare_kernel(half, s_hbm, t_hbm, all_ref, first_ref, second_ref, s_ref, t_ref, sems):
    copies = [
        pltpu.make_async_copy(t_hbm, t_ref, sems.at[1]),
        pltpu.make_async_copy(s_hbm, s_ref, sems.at[0]),
    ]
    for copy in copies:
        copy.start()
    for copy in copies:
        copy.wait()
    sketches = s_ref[...]
    scale = jnp.sqrt(jnp.sum(sketches * sketches, axis=1, keepdims=True) + 1e-06)
    units = (sketches / scale).astype(BF16)
    targets = t_ref[...].T
    hi = targets.astype(BF16).astype(F32)
    mid = (targets - hi).astype(BF16).astype(F32)
    low = targets - hi - mid
    terms = jnp.concatenate([hi, mid, low, jnp.zeros_like(low)], axis=1).astype(BF16)
    all_ref[:, : 2 * half] = units
    all_ref[:, 2 * half :] = terms
    first_ref[:, :half] = units[:, :half]
    first_ref[:, half:] = terms
    second_ref[...] = units[:, half:]


def spans(rows):
    side = 4 * rows
    return [
        pl.ds(at, size)
        for at, size in (
            (0, side),
            (side, side),
            (2 * side, side // 2),
            (5 * side // 2, side // 2),
            (3 * side, side),
        )
    ]


def targets_of(terms, rhs):
    terms = terms.astype(F32).T
    return terms[:rhs] + terms[rhs : 2 * rhs] + terms[2 * rhs : 3 * rhs]


def tile_kernel(rows, rhs, half, at_ref, *refs):
    x_hbm, a_hbm, b_hbm = refs[0], refs[1:6], refs[6:11]
    k_ref, near_ref, far_ref, tx_ref, ty_ref, n0_ref = refs[11:17]
    x_ref, a_ref, b_ref, cos_ref, sems = refs[17:]
    line, quarter, last = 8 * rows, half // 2, half // 4
    dims = (((1,), (1,)), ((), ()))
    plans = (
        (0, quarter, a_hbm, a_ref, 0, quarter),
        (quarter, quarter, a_hbm, a_ref, quarter, quarter + PAD),
        (half, half - last, b_hbm, b_ref, 0, half - last),
        (2 * half - last, last + PAD, b_hbm, b_ref, half - last, last),
    )
    groups = []
    for i, (at_x, wide_x, pieces, ref, at_y, wide_y) in enumerate(plans):
        group = []
        of_x, of_y = pl.ds(at_x, wide_x), pl.ds(at_y, wide_y)
        for core in range(NC):
            of = pl.multiple_of(lax.rem(at_ref[3] + core, NC) * line, line)
            copy = pltpu.make_async_copy(
                x_hbm.at[pl.ds(of, line), of_x],
                x_ref.at[pl.ds(core * line, line), of_x],
                sems.at[i, core],
            )
            group.append(copy)
        for n, (to, piece) in enumerate(zip(spans(rows), pieces)):
            group.append(
                pltpu.make_async_copy(piece.at[:, of_y], ref.at[to, of_y], sems.at[i, NC + n])
            )
        groups.append(group)
        for copy in group:
            copy.start()
    for i, (at_x, wide_x, _, ref, at_y, wide_y) in enumerate(plans):
        for copy in groups[i]:
            copy.wait()
        wide = min(wide_x, wide_y)
        product = lax.dot_general(
            ref[:, at_y : at_y + wide],
            x_ref[:, at_x : at_x + wide],
            dims,
            preferred_element_type=F32,
        )
        to = k_ref if i < 2 else cos_ref
        if i % 2:
            to[...] += product
        else:
            to[...] = product
        if i == 1:
            ty = targets_of(a_ref[:, half:], rhs)
            ty_ref[...] = ty
            n0 = nt(ty, ty)
            n0_ref[...] = n0
            near_ref[:rhs, line:] = n0
            far_ref[:, line:] = n0
    for y in range(4):
        for x in range(4):
            to, of = pl.ds((4 * y + x) * rows, rows), pl.ds((4 * x + y) * rows, rows)
            k_ref[to, :] = jnp.exp(sharpness * (k_ref[to, :] + cos_ref[of, :] - 1.0))
    tx = targets_of(x_ref[:, 2 * half :], rhs)
    tx_ref[...] = tx
    near_ref[rhs:, :line] = tx[:, :line]
    near_ref[rhs:, line:] = jnp.zeros((rhs, rhs), F32)
    product = mm(ty_ref[...], k_ref[...])
    near_ref[:rhs, :line] = product[:, :line]
    far_ref[:, :line] = product[:, line:]


def share_kernel(line, near_ref, far_ref, out_ref, t_ref):
    t_ref[...] = near_ref[far_ref.shape[0] :, :line]
    value = near_ref[: far_ref.shape[0]] + far_ref[...]
    rhs = value.shape[0]
    whole, half = line // 128 * 128, rhs // 2
    rest, gram = value[:, whole:line], value[:, line:]
    parts = [value[:, i : i + 128] for i in range(0, whole, 128)]
    parts.append(jnp.concatenate([rest[:half], rest[half:]], axis=1))
    parts.append(jnp.concatenate([gram[8 * i : 8 * i + 8] for i in range(4)], axis=1))
    at = 0
    for part in parts:
        out_ref[0, at : at + part.shape[0]] = part
        at += part.shape[0]
    dense = out_ref[0]
    for i in range(1, NZ):
        out_ref[i] = dense


def line_kernel(line, part_ref, t_ref, send_ref, n0_ref):
    dense = jnp.sum(part_ref[...], axis=0)
    rhs = send_ref.shape[0]
    whole, half = line // 128, rhs // 2
    parts = [dense[rhs * i : rhs * (i + 1)] for i in range(whole)]
    rest, gram = dense[rhs * whole : rhs * whole + half], dense[rhs * whole + half :]
    parts.append(jnp.concatenate([rest[:, :64], rest[:, 64:]], axis=0))
    t = t_ref[...]
    w = jnp.concatenate(parts, axis=1) - t
    n0_ref[...] = jnp.concatenate([gram[:, rhs * i : rhs * (i + 1)] for i in range(4)], axis=0)
    send_ref[:, :line] = w
    send_ref[:, line : line + rhs] = nt(t, w)
    send_ref[:, line + rhs :] = nt(w, w)


def spread_kernel(rows, line, own_ref, near_ref, far_ref, out_ref):
    out_ref[0, :, :rows] = own_ref[...]
    out_ref[0, :, rows:] = near_ref[:, line:] + far_ref[:, line:]
    payload = out_ref[0]
    for i in range(1, NY * NX):
        out_ref[i] = payload


def eliminate(pairs):
    size = pairs[0][0].shape[0]
    row = lax.broadcasted_iota(jnp.int32, (size, size), 0)
    col = lax.broadcasted_iota(jnp.int32, (size, size), 1)
    pairs = list(pairs)
    block = 8
    for start in range(0, size, block):
        panels = [
            [
                jnp.broadcast_to(m[:, start + j : start + j + 1], (size, size))
                for j in range(block)
            ]
            for m, _ in pairs
        ]
        for j in range(block):
            k = start + j
            for n, (m, c) in enumerate(pairs):
                panel = panels[n]
                inverse = 1.0 / panel[j][k : k + 1, :]
                column = jnp.where(row == k, 0.0, panel[j])
                m_row, c_row = m[k : k + 1, :] * inverse, c[k : k + 1, :] * inverse
                pairs[n] = m - column * m_row, c - column * c_row
                for i in range(j + 1, block):
                    panel[i] = panel[i] - column * (panel[i][k : k + 1, :] * inverse)
    return [
        c / jnp.sum(jnp.where(row == col, m, 0.0), axis=1, keepdims=True) for m, c in pairs
    ]


def symmetric(matrix):
    return 0.5 * (matrix + matrix.T)


def step_kernel(rows, rhs, line, at_ref, *refs):
    got_ref, n0_ref, w_line, w_far, t_tube, t_plane, k_ref = refs[:7]
    out_ref, d_ref, weights_ref, residual_ref, rr_ref, w_ref, d_tube = refs[7:]
    got = jnp.sum(got_ref[...], axis=0)
    n0 = symmetric(n0_ref[...])
    n1, n2 = got[:, rows : rows + rhs], got[:, rows + rhs : rows + 2 * rhs]
    y, x = at_ref[1], at_ref[2]
    for dy in range(NY):
        for dx in range(NX):
            s = NX * dy + dx
            of = lax.rem(y + dy, NY) * NX + lax.rem(x + dx, NX)
            w_ref[:, s * rows : (s + 1) * rows] = got_ref[of][:, :rows]
    eye = (
        lax.broadcasted_iota(jnp.int32, (rhs, rhs), 0)
        == lax.broadcasted_iota(jnp.int32, (rhs, rhs), 1)
    ).astype(F32)
    a1, n0_inverse = eliminate([(symmetric(n1) + 2.0 * n0, n0), (n0, eye)])
    a1t = a1.T
    q = eye - 2.0 * a1
    qt = eye - 2.0 * a1t
    cross = mm(qt, mm(n1, a1))
    rr1 = mm(qt, mm(n0, q)) - cross - cross.T + mm(a1t, mm(n2, a1))
    mix = qt + mm(n0_inverse, rr1).T
    d_plane = mm(mix, t_plane[...]) - mm(a1t, w_ref[...])
    d_tube[:, :line] = mm(mix, t_tube[:, :line]) - mm(a1t, w_line[:, :line])
    d_tube[:, line:] = mm(mix, t_tube[:, line:]) - mm(a1t, w_far[:, :line])
    product = nt(d_tube[...], k_ref[...])
    d_own, t_own = d_plane[:, :rows], t_plane[:, :rows]
    gram = nt(d_plane, product) + nt(d_own, d_own)
    for dy in range(NY):
        for dx in range(NX):
            s = NX * dy + dx
            of = lax.rem(y + dy, NY) * NX + lax.rem(x + dx, NX)
            block = product[:, s * rows : (s + 1) * rows]
            out_ref[of] = jnp.concatenate([block, gram], axis=1)
    d_ref[...] = d_own
    weights_ref[...] = mm(a1t, t_own)
    residual_ref[...] = mm(qt, t_own) - mm(a1t, w_ref[:, :rows])
    rr_ref[...] = rr1


def image_kernel(rows, got_ref, d_ref, image_ref, out_ref):
    got = jnp.sum(got_ref[...], axis=0)
    image_ref[...] = got[:, :rows] + d_ref[...]
    gram = got[:, rows:]
    dense = jnp.concatenate([gram[8 * i : 8 * i + 8] for i in range(4)], axis=1)
    for i in range(NZ * NC):
        out_ref[i] = dense


def last_kernel(rhs, got_ref, rr, d_own, image, weights, residual, out_weights, out_residual):
    dense = jnp.sum(got_ref[...], axis=0)
    gram = jnp.concatenate([dense[:, rhs * i : rhs * (i + 1)] for i in range(4)], axis=0)
    (a2,) = eliminate([(symmetric(gram), rr[...])])
    a2t = a2.T
    out_weights[...] = weights[...] + mm(a2t, d_own[...])
    out_residual[...] = residual[...] - mm(a2t, image[...])


def local(sketches, targets):
    rows, rhs = targets.shape
    half = sketches.shape[1] // 2
    line, plane = NZ * rows, NY * NX * rows
    z = lax.axis_index("row") // 4
    y = lax.axis_index("row") // 2 % 2 + 2 * (lax.axis_index("col") // NX)
    x = lax.axis_index("col") % NX
    c = lax.axis_index("row") % NC
    at = jnp.stack([z, y, x, c]).astype(jnp.int32)
    sizes = (rows, rhs, half)

    units, first, second = small_kernel(
        functools.partial(prepare_kernel, half),
        (
            shape(rows, 2 * half + PAD, dtype=BF16),
            shape(rows, half + PAD, dtype=BF16),
            shape(rows, half, dtype=BF16),
        ),
        (sketches, targets.T),
        [HBM] * 2,
        limit=60,
        scratch=[
            pltpu.VMEM((rows, 2 * half), F32),
            pltpu.VMEM((rhs, rows), F32),
            pltpu.SemaphoreType.DMA((2,)),
        ],
        name="prepare",
    )
    tube = lax.all_gather(units, AXES, axis=0, tiled=True, axis_index_groups=TUBES)
    a = jnp.concatenate([first] + [from_x(first, k) for k in range(1, NX)], axis=0)
    b = jnp.concatenate([second] + [from_y(second, k) for k in range(1, NY)], axis=0)
    a, b = lax.optimization_barrier((a, b))
    a1, b1, a3, b3 = from_y(a, 1), from_x(b, 1), from_y(a, 3), from_x(b, 3)
    top = 2 * rows
    a2, b2 = from_y(a1[:top], 1), from_x(b1[:top], 1)
    a2_low, b2_low = from_y(a3[top:], 3), from_x(b3[top:], 3)
    a, b = (a, a1, a2, a2_low, a3), (b, b1, b2, b2_low, b3)
    k, near, far, t_tube, t_plane, n0 = pl.pallas_call(
        functools.partial(tile_kernel, *sizes),
        out_shape=(
            shape(plane, NC * line),
            shape(2 * rhs, line + rhs),
            shape(rhs, line + rhs),
            shape(rhs, NC * line),
            shape(rhs, plane),
            shape(rhs, rhs),
        ),
        in_specs=[SM] + [HBM] * 11,
        out_specs=[VM] * 6,
        scratch_shapes=[
            pltpu.VMEM((NC * line, 2 * half + PAD), BF16),
            pltpu.VMEM((plane, half + PAD), BF16),
            pltpu.VMEM((plane, half), BF16),
            pltpu.VMEM((plane, NC * line), F32),
            pltpu.SemaphoreType.DMA((4, NC + 5)),
        ],
        compiler_params=pltpu.CompilerParams(vmem_limit_bytes=52 * MIB),
        cost_estimate=pl.CostEstimate(
            flops=4 * plane * NC * line * 2 * half,
            bytes_accessed=2 * (plane + NC * line) * 2 * half,
            transcendentals=plane * NC * line,
        ),
        name="tile",
    )(at, tube, *a, *b)

    copies, t_line = small_kernel(
        functools.partial(share_kernel, line),
        (shape(NZ, rhs * (line + rhs) // 128, 128), shape(rhs, line)),
        (near, other_core(far)),
        name="share",
    )
    sent, n0 = small_kernel(
        functools.partial(line_kernel, line),
        (shape(rhs, line + 2 * rhs), shape(rhs, rhs)),
        (exchange(copies, LINES), t_line),
        name="line",
    )
    w_own = lax.dynamic_slice(sent, (0, z * rows), (rhs, rows))
    received = other_core(sent)
    copies = small_kernel(
        functools.partial(spread_kernel, rows, line),
        shape(NY * NX, rhs, rows + 2 * rhs),
        (w_own, sent, received),
        name="spread",
    )
    got = exchange(copies, PLANES)
    own = shape(rhs, rows)
    values = (at, got, n0, sent, received, t_tube, t_plane, k)
    chunks, d_own, weights, residual, rr1 = small_kernel(
        functools.partial(step_kernel, rows, rhs, line),
        (shape(NY * NX, rhs, rows + rhs), own, own, own, shape(rhs, rhs)),
        values,
        [SM] + [VM] * 7,
        limit=16,
        scratch=[pltpu.VMEM((rhs, plane), F32), pltpu.VMEM((rhs, NC * line), F32)],
        name="step",
    )
    image, copies = small_kernel(
        functools.partial(image_kernel, rows),
        (own, shape(NZ * NC, rhs // 4, 4 * rhs)),
        (exchange(chunks, PLANES), d_own),
        name="image",
    )
    weights, residual = small_kernel(
        functools.partial(last_kernel, rhs),
        (own, own),
        (exchange(copies, TUBES), rr1, d_own, image, weights, residual),
        name="last",
    )
    return weights.T, residual.T


def solution(mesh):
    in_specs = (P(AXES, None), P(AXES, None))
    out_specs = (P(AXES, None), P(AXES, None))
    return jax.shard_map(local, mesh=mesh, in_specs=in_specs, out_specs=out_specs, check_vma=False)
```
